128 devices in a mesh: blk: 32 (over x, z, y_lo), rep: 4 (over y_hi, core).
Axes of the slice: x: 4, y: 4 (y_hi: 2, y_lo: 2; y = y_hi * 2 + y_lo), z: 4, core: 2. Of those that a mesh axis runs over, the one named last changes fastest.
Arguments:
- points: float32 [32, 32768], P(None, 'blk'), may hold values from -6 to 6
- lengthscale: float32 [32], replicated, may hold values from 1.5 to 6
- noise: float32 [1], replicated, may hold values from 0.5 to 2
- solution: float32 [16, 32768], P('rep', 'blk'), may hold values from -6 to 6
- residual: float32 [16, 32768], P('rep', 'blk'), may hold values from -11 to 11
- direction: float32 [16, 32768], P('rep', 'blk'), may hold values from -6 to 6
Outputs:
- new_solution: float32 [16, 32768], P('rep', 'blk')
- new_residual: float32 [16, 32768], P('rep', 'blk')
- new_direction: float32 [16, 32768], P('rep', 'blk')
The draws below stay inside these ranges and needn't reach their ends.
All inputs are finite; a program needn't handle non-finite values.
Results may differ from the reference program's by a relative error of at most 0.035.
Values may be sent and summed in bfloat16 or wider, within the bound.
A program may use at most 64 MiB of HBM per device.

```python
import math
import jax
import jax.numpy as jnp
from jax import lax

FEATURES = 32
PROBES = 16
NPTS = 32768


def draw_residual(key, part):
    key = jax.random.fold_in(key, 7)
    ramp = jnp.sqrt(1.0 + 2.0 * jnp.arange(NPTS, dtype=jnp.float32) / NPTS)
    base = jnp.clip(jax.random.normal(key, (PROBES, NPTS), jnp.float32), -6.0, 6.0)
    return (base * ramp[None, :]).astype(jnp.float32)


def steps_of(key, shape, split, least, high):
    def one(dim, blocks):
        draws = jax.random.uniform(jax.random.fold_in(jax.random.fold_in(key, 6), dim), (blocks,), jnp.float32, least / len(split), high / len(split))
        return jnp.repeat(jnp.exp(draws), shape[dim] // blocks).reshape((-1,) + (1,) * (len(shape) - dim - 1))

    loudness = one(*split[0])
    for cut in split[1:]:
        loudness = loudness * one(*cut)
    return loudness


def normal_values(key, dims, spread, reach, cuts=(), held_as=jnp.bfloat16):
    result = jax.random.normal(key, dims, jnp.float32) * spread
    if len(cuts) > 0:
        result = steps_of(key, dims, cuts, -0.22, 0.18) * result
    return jnp.clip(result, min=-reach, max=reach).astype(held_as)


def setup_inputs(seed: int = 0) -> dict:
    key_list = jax.random.split(jax.random.key(seed), 7)
    return {
        "points": normal_values(key_list[0], (FEATURES, NPTS), 1.0, 6.0, ((1, 32),), jnp.float32),
        "lengthscale": jnp.clip(jnp.exp(jax.random.uniform(key_list[1], (FEATURES,), jnp.float32, math.log(1.5), math.log(6.0))), 1.5, 6.0),
        "noise": jnp.clip(jax.random.uniform(key_list[2], (1,), jnp.float32, 0.5, 2.0), 0.5, 2.0),
        "solution": normal_values(key_list[3], (PROBES, NPTS), 1.0, 6.0, ((0, 4), (1, 32)), jnp.float32),
        "residual": draw_residual(jax.random.fold_in(key_list[6], 71), 0),
        "direction": normal_values(key_list[5], (PROBES, NPTS), 1.0, 6.0, ((0, 4), (1, 32)), jnp.float32),
    }


root_five = math.sqrt(5.0)

def matern(dist2):
    radius = jnp.sqrt(dist2)
    return (1.0 + root_five * radius + 5.0 / 3.0 * dist2) * jnp.exp(-root_five * radius)

def reference(points, lengthscale, noise, solution, residual, direction):
    scaled = (points / lengthscale[:, None]).astype(jnp.bfloat16)
    wide = scaled.astype(jnp.float32)
    sq_norms = lax.optimization_barrier(jnp.sum(wide * wide, axis=0))
    dir_wide = direction.astype(jnp.bfloat16).astype(jnp.float32)
    block = math.gcd(NPTS, 2048)
    count = NPTS // block

    def add_block(total, index):
        start = (index * block).astype(jnp.int32)
        cols = lax.dynamic_slice_in_dim(wide, start, block, 1)
        col_sq = lax.dynamic_slice_in_dim(sq_norms, start, block, 0)
        cross = jnp.dot(wide.T, cols, precision=lax.Precision.HIGHEST)
        dist2 = jnp.maximum(sq_norms[:, None] + col_sq[None, :] - 2.0 * cross, 0.0)
        kernel = matern(dist2).astype(jnp.bfloat16).astype(jnp.float32)
        dir_cols = lax.dynamic_slice_in_dim(dir_wide, start, block, 1)
        return (total + jnp.dot(dir_cols, kernel.T, precision=lax.Precision.HIGHEST), None)
    zeros = jnp.zeros((PROBES, NPTS), jnp.float32)
    product, unused = lax.scan(add_block, zeros, jnp.arange(count, dtype=jnp.int32))
    image = product + noise[0] * direction
    rr_old = lax.optimization_barrier(jnp.sum(residual * residual, axis=1))
    curv = lax.optimization_barrier(jnp.sum(direction * image, axis=1))
    alpha = rr_old / curv
    new_solution = solution + alpha[:, None] * direction
    new_residual = residual - alpha[:, None] * image
    rr_new = lax.optimization_barrier(jnp.sum(new_residual * new_residual, axis=1))
    new_direction = new_residual + (rr_new / rr_old)[:, None] * direction
    return (new_solution, new_residual, new_direction)
```

```python
import math

import jax
import jax.numpy as jnp
from jax import lax
from jax.experimental import pallas as pl
from jax.experimental.pallas import tpu as pltpu
from jax.sharding import PartitionSpec as P

MESH = pl.DeviceIdType.MESH
bf16 = jnp.bfloat16
f32 = jnp.float32
BLOCK = 1024
TILE = 512
OFFSETS = ((0, 1), (1, 0), (1, 1), (1, 3), (1, 2), (2, 1), (2, 2), (0, 2), (2, 0))
SCALE = math.sqrt(5.0) / 3.0


def matern(dist):
    dist = jnp.maximum(dist, 1e-30)
    root = dist * lax.rsqrt(dist)
    decay = jnp.exp2(root * (-3.0 / math.log(2.0)))
    return ((root + dist + 1.0 / 3.0) * decay).astype(bf16)


def pick(index, values):
    result = jnp.int32(values[0])
    for k in range(1, len(values)):
        result = jnp.where(index == k, jnp.int32(values[k]), result)
    return result


def squares(points):
    wide = points.astype(f32)
    total = jnp.sum(wide * wide, axis=0, keepdims=True)
    high = total.astype(bf16).astype(f32)
    rest = total - high
    mid = rest.astype(bf16).astype(f32)
    return (high, mid, rest - mid)


def kernel(
    points_ref, length_ref, noise_ref, sol_ref, res_ref, dir_ref,
    out_sol, out_res, out_dir,
    pts, dirs, dmat, amat, first, second, parts, got, sums1, sums2,
    pts_send, pts_recv, dir_send, dir_recv, part_send, part_recv, sum_send, sum_recv,
):
    blk = lax.axis_index("blk")
    rep = lax.axis_index("rep")
    ylo = blk % 2
    col = blk // 2
    x = col // 4
    z = col % 4
    me = ylo * 4 + rep
    dx1 = pick(me, [d[0] for d in OFFSETS[:8]])
    dz1 = pick(me, [d[1] for d in OFFSETS[:8]])
    dx2, dz2 = OFFSETS[8]

    def column(dx, dz):
        return ((x + dx + 4) % 4) * 4 + (z + dz + 4) % 4

    def member(c, k):
        return (c * 2 + k // 4, k % 4)

    other1 = column(dx1, dz1)
    other2 = column(dx2, dz2)
    mates = [member(col, (me + m) % 8) for m in range(1, 8)]
    users = [member(column(-d[0], -d[1]), min(k, 7)) for k, d in enumerate(OFFSETS)]
    peers1 = []
    for m in range(1, 8):
        e = (x * 2 + ylo + m) % 8
        peers1.append((((e // 2) * 4 + z) * 2 + e % 2, rep))
    peers2 = [((x * 4 + (z + m) % 4) * 2 + ylo, rep) for m in range(1, 4)]

    barrier = pltpu.get_barrier_semaphore()
    sources1 = [member(other1, k) for k in range(8)]
    sources2 = [member(other2, k) for k in range(8)]

    def hail(device):
        pl.semaphore_signal(barrier, inc=1, device_id=device, device_id_type=MESH)

    for device in mates + users + sources1 + peers1 + peers2:
        hail(device)

    @pl.when(me == 7)
    def _():
        for device in sources2:
            hail(device)

    row = lax.broadcasted_iota(jnp.int32, (32, 32), 0)
    lane = lax.broadcasted_iota(jnp.int32, (32, 32), 1)
    length = jnp.sum(jnp.where(row == lane, length_ref[...], 0.0), axis=1, keepdims=True)
    pts[ylo, 0:32, :] = (points_ref[...] * (SCALE / length)).astype(bf16)
    direction = dir_ref[...]
    dirs[me] = jnp.concatenate(
        [direction[:, c * 256 : (c + 1) * 256] for c in range(4)], axis=0
    ).astype(bf16)

    pl.semaphore_wait(barrier, 34 + 8 * jnp.where(me == 7, 1, 0))

    def send(src, dst, send_sem, recv_sem, device):
        copy = pltpu.make_async_remote_copy(
            src_ref=src, dst_ref=dst, send_sem=send_sem, recv_sem=recv_sem,
            device_id=device, device_id_type=MESH,
        )
        copy.start()
        return copy

    def send_points(slot, device, k):
        place = slot * 2 + ylo
        return send(
            pts.at[ylo, pl.ds(0, 32)], pts.at[place, pl.ds(0, 32)], pts_send.at[k], pts_recv.at[place], device
        )

    def user_of(k):
        return member(column(-pick(k, [d[0] for d in OFFSETS[:8]]), -pick(k, [d[1] for d in OFFSETS[:8]])), k)

    waits = []
    waits.append(send_points(0, (blk + 1 - 2 * ylo, rep), 0))
    waits.append(send_points(1, user_of(rep), 1))
    waits.append(send_points(1, user_of(rep + 4), 2))

    @pl.when(rep == 0)
    def _():
        send_points(2, users[8], 3)

    for m in range(7):
        waits.append(send(dirs.at[me], dirs.at[me], dir_send.at[m], dir_recv.at[me], mates[m]))
    for k in range(9):
        place = (1 if k < 8 else 2) * 8 + me
        waits.append(send(dirs.at[me], dirs.at[place], dir_send.at[7 + k], dir_recv.at[place], users[k]))

    first[...] = jnp.zeros_like(first)
    second[...] = jnp.zeros_like(second)

    def take_points(place):
        pltpu.make_async_copy(pts.at[place, pl.ds(0, 32)], pts.at[place, pl.ds(0, 32)], pts_recv.at[place]).wait()

    def take_dirs(place):
        pltpu.make_async_copy(dirs.at[place], dirs.at[place], dir_recv.at[place]).wait()

    def augment(place):
        high, mid, low = squares(pts[place, 0:32, :])
        one = jnp.ones((1, BLOCK), f32)
        extra = jnp.concatenate([high, mid, low, one, one, one, jnp.zeros((10, BLOCK), f32)], axis=0)
        pts[place, 32:48, :] = extra.astype(bf16)

    def own_rows(place):
        q = pts[place, 0:32, :]
        high, mid, low = squares(q)
        one = jnp.ones((1, BLOCK), f32)
        whole = jnp.concatenate(
            [q.astype(f32) * -2.0, one, one, one, high, mid, low, jnp.zeros((10, BLOCK), f32)], axis=0
        )
        amat[place] = jnp.transpose(whole).astype(bf16)

    def spread(place):
        pieces = [dirs[place * 4 + r].astype(f32) for r in range(4)]
        for c in range(4):
            rows = jnp.concatenate([p[c * 4 : c * 4 + 4, :] for p in pieces], axis=0)
            dmat[place, :, c * 256 : (c + 1) * 256] = rows.astype(bf16)

    take_points(1 - ylo)
    for place in range(2):
        augment(place)
        own_rows(place)
    for m in range(1, 8):
        take_dirs((me + m) % 8)
    for place in range(2):
        spread(place)

    def arrive(slot):
        for y in range(2):
            take_points(slot * 2 + y)
            augment(slot * 2 + y)
        for k in range(8):
            take_dirs(slot * 8 + k)
        for y in range(2):
            spread(slot * 2 + y)

    arrive(1)

    @pl.when(me == 7)
    def _():
        arrive(2)

    early1 = jnp.where(col < other1, 0, 2)
    early2 = jnp.where(col < other2, 0, 2)

    def half(u, early):
        i = jnp.where(u < 4, 0, early) + (u // 2) % 2
        j = jnp.where(u < 4, 2, early) + u % 2
        return i, j

    def tile(t):
        hi, hj = half(t % 8, jnp.where(t < 8, early1, early2))
        v = t - 8
        w = v - 4
        di = jnp.where(v < 4, v, jnp.where(w < 3, 0, jnp.where(w < 5, 1, 2)))
        dj = jnp.where(v < 4, v, jnp.where(w < 3, w + 1, jnp.where(w < 5, w - 1, 3)))
        diag = jnp.logical_and(me == 6, t >= 8)
        i = jnp.where(me < 6, t // 4, jnp.where(diag, di, hi))
        j = jnp.where(me < 6, 4 + t % 4, jnp.where(diag, dj, jnp.where(t < 8, 4, 8) + hj))
        same = jnp.logical_and(diag, v < 4)
        return i, j, same

    def step(t, carry):
        i, j, same = tile(t)
        ib, i0 = i // 2, pl.multiple_of((i % 2) * TILE, TILE)
        jb, j0 = j // 2, pl.multiple_of((j % 2) * TILE, TILE)
        dist = jnp.dot(
            amat[ib, pl.ds(i0, TILE), :], pts[jb, :, pl.ds(j0, TILE)], preferred_element_type=f32
        )
        values = matern(dist)
        weight = jnp.where(same, 0.5, 1.0).astype(bf16)
        di = dmat[ib, :, pl.ds(i0, TILE)] * weight
        dj = dmat[jb, :, pl.ds(j0, TILE)] * weight
        first[ib, :, pl.ds(i0, TILE)] += lax.dot_general(
            dj, values, (((1,), (1,)), ((), ())), preferred_element_type=f32
        )
        second[jb, :, pl.ds(j0, TILE)] += jnp.dot(di, values, preferred_element_type=f32)
        return carry

    lax.fori_loop(0, 16 + 2 * jnp.where(me == 6, 1, 0), step, 0)

    def pack(place, whole):
        for r in range(4):
            piece = [whole[r * 4 : r * 4 + 4, c * 256 : (c + 1) * 256] for c in range(4)]
            parts[place * 4 + r] = jnp.concatenate(piece, axis=0).astype(bf16)

    for y in range(2):
        pack(2 + y, second[2 + y])
    for k in range(8):
        waits.append(send(parts.at[8 + k], got.at[8 + me], part_send.at[8 + k], part_recv.at[8 + me], sources1[k]))

    @pl.when(me == 7)
    def _():
        for y in range(2):
            pack(4 + y, second[4 + y])
        for k in range(8):
            send(parts.at[16 + k], got.at[16], part_send.at[16 + k], part_recv.at[16], sources2[k])

    for y in range(2):
        pack(y, first[y] + second[y])
    for m in range(7):
        k = (me + m + 1) % 8
        waits.append(send(parts.at[k], got.at[me], part_send.at[k], part_recv.at[me], mates[m]))

    total = parts[me].astype(f32)
    for k in range(17):
        def take_part():
            pltpu.make_async_copy(got.at[k], got.at[k], part_recv.at[k]).wait()
        if k < 8:
            got_k = (me + k) % 8
            if k == 0:
                continue
            pltpu.make_async_copy(got.at[got_k], got.at[got_k], part_recv.at[got_k]).wait()
            total += got[got_k].astype(f32)
        else:
            take_part()
            total += got[k].astype(f32)

    product = jnp.concatenate([total[c * 4 : c * 4 + 4, :] for c in range(4)], axis=1)
    image = 3.0 * product + noise_ref[0] * direction
    residual = res_ref[...]

    def lanes(a):
        result = a[:, 0:128]
        for c in range(1, 8):
            result += a[:, c * 128 : (c + 1) * 128]
        return result

    e = x * 2 + ylo
    sums1[e] = jnp.concatenate(
        [lanes(residual * residual), lanes(direction * image), lanes(residual * image), lanes(image * image)], axis=0
    )
    for m in range(7):
        waits.append(send(sums1.at[e], sums1.at[e], sum_send.at[m], sum_recv.at[e], peers1[m]))
    for m in range(1, 8):
        place = (e + m) % 8
        pltpu.make_async_copy(sums1.at[place], sums1.at[place], sum_recv.at[place]).wait()
    sums2[z] = sum(sums1[k] for k in range(8))
    for m in range(3):
        waits.append(send(sums2.at[z], sums2.at[z], sum_send.at[7 + m], sum_recv.at[8 + z], peers2[m]))
    for m in range(1, 4):
        place = (z + m) % 4
        pltpu.make_async_copy(sums2.at[place], sums2.at[place], sum_recv.at[8 + place]).wait()
    stats = jnp.sum(sum(sums2[k] for k in range(4)), axis=1, keepdims=True)
    rr, curv, cross, norm = stats[0:4], stats[4:8], stats[8:12], stats[12:16]
    alpha = rr / curv
    rr_new = jnp.maximum(rr - 2.0 * alpha * cross + alpha * alpha * norm, 0.0)
    new_res = residual - alpha * image
    out_sol[...] = sol_ref[...] + alpha * direction
    out_res[...] = new_res
    out_dir[...] = new_res + (rr_new / rr) * direction

    for copy in waits:
        copy.wait_send()

    @pl.when(rep == 0)
    def _():
        pltpu.make_async_copy(pts.at[0, pl.ds(0, 32)], pts.at[0, pl.ds(0, 32)], pts_send.at[3]).wait()

    @pl.when(me == 7)
    def _():
        for k in range(8):
            pltpu.make_async_copy(parts.at[k], parts.at[k], part_send.at[16 + k]).wait()


def on_device(points, lengthscale, noise, solution, residual, direction):
    vmem = pl.BlockSpec(memory_space=pltpu.VMEM)
    dma = pltpu.SemaphoreType.DMA
    return pl.pallas_call(
        kernel,
        out_shape=[jax.ShapeDtypeStruct(direction.shape, f32)] * 3,
        in_specs=[vmem, vmem, pl.BlockSpec(memory_space=pltpu.SMEM), vmem, vmem, vmem],
        out_specs=[vmem] * 3,
        scratch_shapes=[
            pltpu.VMEM((6, 48, BLOCK), bf16),
            pltpu.VMEM((24, 16, 256), bf16),
            pltpu.VMEM((6, 16, BLOCK), bf16),
            pltpu.VMEM((2, BLOCK, 48), bf16),
            pltpu.VMEM((2, 16, BLOCK), f32),
            pltpu.VMEM((6, 16, BLOCK), f32),
            pltpu.VMEM((24, 16, 256), bf16),
            pltpu.VMEM((17, 16, 256), bf16),
            pltpu.VMEM((8, 16, 128), f32),
            pltpu.VMEM((4, 16, 128), f32),
            dma((4,)), dma((6,)), dma((16,)), dma((24,)), dma((24,)), dma((17,)), dma((10,)), dma((12,)),
        ],
        compiler_params=pltpu.CompilerParams(
            collective_id=0, has_side_effects=True, vmem_limit_bytes=40 * 2**20
        ),
        cost_estimate=pl.CostEstimate(flops=2**31, bytes_accessed=2**20, transcendentals=2**23),
    )(points, lengthscale.reshape(1, 32), noise, solution, residual, direction)


def solution(mesh):
    in_specs = (P(None, "blk"), P(), P(), P("rep", "blk"), P("rep", "blk"), P("rep", "blk"))
    out_specs = (P("rep", "blk"), P("rep", "blk"), P("rep", "blk"))
    return jax.shard_map(
        on_device, mesh=mesh, in_specs=in_specs, out_specs=out_specs, check_vma=False
    )
```

```python
import math

import jax
import jax.numpy as jnp
from jax import lax
from jax.experimental import pallas as pl
from jax.experimental.pallas import tpu as pltpu
from jax.sharding import PartitionSpec as P

MESH = pl.DeviceIdType.MESH
bf16 = jnp.bfloat16
f32 = jnp.float32
BLOCK = 1024
ROWS = 512
COLS = 256
SCALE = math.sqrt(5.0) / 3.0
SLOTS = (
    ((0, 0), (0, 1), None, None),
    ((0, 0), (1, 0), None, None),
    ((-1, 0), (0, 1), None, None),
    ((-1, 0), (0, -1), None, None),
    ((0, -1), (1, 1), None, None),
    ((-1, 0), (1, 1), None, None),
    ((0, 0), None, (-1, -1), (1, 1)),
    ((0, -1), (0, 1), (-1, 0), (1, 0)),
)
USES = tuple((m, s) + SLOTS[m][s] for m in range(8) for s in range(4) if SLOTS[m][s] is not None)


def use_of(m, s):
    for index, use in enumerate(USES):
        if use[:2] == (m, s):
            return index
    return 0


def matern(dist):
    dist = jnp.maximum(dist, 1e-30)
    root = dist * lax.rsqrt(dist)
    decay = jnp.exp2(root * (-3.0 / math.log(2.0)))
    return ((root + dist + 1.0 / 3.0) * decay).astype(bf16)


def pick(index, values):
    result = jnp.int32(values[0])
    for k in range(1, len(values)):
        if values[k] != values[0]:
            result = jnp.where(index == k, jnp.int32(values[k]), result)
    return result


def squares(points):
    wide = points.astype(f32)
    total = jnp.sum(wide * wide, axis=0, keepdims=True)
    high = total.astype(bf16).astype(f32)
    rest = total - high
    mid = rest.astype(bf16).astype(f32)
    return (high, mid, rest - mid)


def kernel(
    points_hbm, length_hbm, noise_hbm, sol_hbm, res_hbm, dir_hbm,
    out_sol, out_res, out_dir,
    points_ref, length_ref, noise_ref, sol_ref, res_ref, dir_ref,
    mine, mydir, pts, dirs, dmat, amat, even, odd, first, second, parts, got, sums,
    load, pts_send, pts_recv, dir_send, dir_recv, part_send, part_recv, sum_send, sum_recv,
):
    loads = [
        pltpu.make_async_copy(a, b, load.at[n])
        for n, (a, b) in enumerate(
            [
                (points_hbm, points_ref), (length_hbm, length_ref), (dir_hbm, dir_ref),
                (noise_hbm, noise_ref), (sol_hbm, sol_ref), (res_hbm, res_ref),
            ]
        )
    ]
    for copy in loads:
        copy.start()

    blk = lax.axis_index("blk")
    rep = lax.axis_index("rep")
    ylo = blk % 2
    col = blk // 2
    x = col // 4
    z = col % 4
    me = ylo * 4 + rep

    def column(dx, dz):
        return ((x + dx + 4) % 4) * 4 + (z + dz + 4) % 4

    def member(c, k):
        return (c * 2 + k // 4, k % 4)

    def slot_column(s):
        offsets = [SLOTS[m][s] or (0, 0) for m in range(8)]
        return column(pick(me, [d[0] for d in offsets]), pick(me, [d[1] for d in offsets]))

    slot_cols = [slot_column(s) for s in range(4)]
    slot_use = [pick(me, [use_of(m, s) for m in range(8)]) for s in range(4)]
    own_pair = jnp.logical_or(jnp.logical_or(me == 0, me == 1), me == 6)
    users = [member(column(-dx, -dz), m) for m, s, dx, dz in USES]
    peers = [((blk + m) % 32, rep) for m in range(1, 32)]

    barrier = pltpu.get_barrier_semaphore()

    def hail(device):
        pl.semaphore_signal(barrier, inc=1, device_id=device, device_id_type=MESH)

    def if_slot(s, action):
        if s == 0:
            action()
        elif s == 1:
            pl.when(me != 6)(action)
        else:
            pl.when(me >= 6)(action)

    def hail_sources(s):
        def action():
            for k in range(8):
                if s == 0:
                    @pl.when(jnp.logical_not(jnp.logical_and(own_pair, me == k)))
                    def _():
                        hail(member(slot_cols[s], k))
                else:
                    hail(member(slot_cols[s], k))
        return action

    for s in range(4):
        if_slot(s, hail_sources(s))
    for use, device in zip(USES, users):
        if use[2:] == (0, 0):
            @pl.when(me != use[0])
            def _():
                hail(device)
        else:
            hail(device)
    for device in peers:
        hail(device)

    for copy in loads[:3]:
        copy.wait()
    row = lax.broadcasted_iota(jnp.int32, (32, 32), 0)
    lane = lax.broadcasted_iota(jnp.int32, (32, 32), 1)
    length = jnp.sum(jnp.where(row == lane, length_ref[...], 0.0), axis=1, keepdims=True)
    mine[...] = (points_ref[...] * (SCALE / length)).astype(bf16)
    direction = dir_ref[...]
    mydir[...] = jnp.concatenate(
        [direction[:, c * 256 : (c + 1) * 256] for c in range(4)], axis=0
    ).astype(bf16)

    slots_used = jnp.where(me < 6, 2, jnp.where(me == 6, 3, 4))
    pl.semaphore_wait(barrier, 8 * slots_used + len(USES) + 31 - 2 * jnp.where(own_pair, 1, 0))

    def remote(src, dst, send_sem, recv_sem, device):
        return pltpu.make_async_remote_copy(
            src_ref=src, dst_ref=dst, send_sem=send_sem, recv_sem=recv_sem,
            device_id=device, device_id_type=MESH,
        )

    def deliver(src, dst, send_sem, recv_sem, device, is_self, start):
        def away():
            copy = remote(src, dst, send_sem, recv_sem, device)
            copy.start() if start else copy.wait_send()

        def here():
            if start:
                pltpu.make_async_copy(src, dst, recv_sem).start()

        if is_self is None:
            away()
        else:
            pl.when(is_self)(here)
            pl.when(jnp.logical_not(is_self))(away)

    def points_out(start):
        for r in range(4):
            @pl.when(rep == r)
            def _():
                index = 0
                for u, (m, s, dx, dz) in enumerate(USES):
                    if m % 4 == r:
                        place = s * 2 + ylo
                        deliver(
                            mine, pts.at[place, pl.ds(0, 32)], pts_send.at[index], pts_recv.at[place], users[u],
                            me == m if (dx, dz) == (0, 0) else None, start,
                        )
                        index += 1

    def dirs_out(start):
        for u, (m, s, dx, dz) in enumerate(USES):
            place = s * 8 + me
            deliver(
                mydir, dirs.at[place], dir_send.at[u], dir_recv.at[place], users[u],
                me == m if (dx, dz) == (0, 0) else None, start,
            )

    points_out(True)
    dirs_out(True)
    first[...] = jnp.zeros_like(first)
    second[...] = jnp.zeros_like(second)

    def augment(place):
        pltpu.make_async_copy(pts.at[place, pl.ds(0, 32)], pts.at[place, pl.ds(0, 32)], pts_recv.at[place]).wait()
        high, mid, low = squares(pts[place, 0:32, :])
        one = jnp.ones((1, BLOCK), f32)
        extra = jnp.concatenate([high, mid, low, one, one, one, jnp.zeros((10, BLOCK), f32)], axis=0)
        pts[place, 32:48, :] = extra.astype(bf16)

    def left_rows(place, y):
        q = pts[place, 0:32, :]
        high, mid, low = squares(q)
        one = jnp.ones((1, BLOCK), f32)
        whole = jnp.concatenate(
            [q.astype(f32) * -2.0, one, one, one, high, mid, low, jnp.zeros((10, BLOCK), f32)], axis=0
        )
        amat[y] = jnp.transpose(whole).astype(bf16)

    def spread(place):
        pieces = []
        for r in range(4):
            k = place * 4 + r
            pltpu.make_async_copy(dirs.at[k], dirs.at[k], dir_recv.at[k]).wait()
            pieces.append(dirs[k].astype(f32))
        for c in range(4):
            rows = jnp.concatenate([p[c * 4 : c * 4 + 4, :] for p in pieces], axis=0)
            dmat[place, :, c * 256 : (c + 1) * 256] = rows.astype(bf16)

    def pack(place, whole):
        for r in range(4):
            piece = [whole[r * 4 : r * 4 + 4, c * 256 : (c + 1) * 256] for c in range(4)]
            parts[place * 4 + r] = jnp.concatenate(piece, axis=0).astype(bf16)

    def parts_out(s, start):
        def action():
            for k in range(8):
                deliver(
                    parts.at[s * 8 + k], got.at[slot_use[s]], part_send.at[s * 8 + k], part_recv.at[slot_use[s]],
                    member(slot_cols[s], k), jnp.logical_and(own_pair, me == k) if s == 0 else None, start,
                )
        return action

    def phase(ph, carry):
        diag = jnp.logical_and(me == 6, ph == 0)
        left = ph * 4
        right = jnp.where(diag, 0, ph * 4 + 2)
        for y in range(2):
            augment(left + y)
            left_rows(left + y, y)

        @pl.when(jnp.logical_not(diag))
        def _():
            for y in range(2):
                augment(right + y)

        for y in range(2):
            spread(left + y)

        @pl.when(jnp.logical_not(diag))
        def _():
            for y in range(2):
                spread(right + y)

        low_col = jnp.where(ph == 0, slot_cols[0], slot_cols[2])
        high_col = jnp.where(ph == 0, slot_cols[1], slot_cols[3])
        early = jnp.where(low_col < high_col, 0, 1)
        count = jnp.where(me < 6, 32, jnp.where(diag, 20, 16))

        def tile(t):
            u = t - 8
            half_i = jnp.where(t < 8, t // 4, 2 * early + u // 4)
            half_j = jnp.where(t < 8, 4 + t % 4, 4 * early + t % 4)
            v = t // 2
            w = v - 4
            diag_i = jnp.where(v < 4, v, jnp.where(w < 3, 0, jnp.where(w < 5, 1, 2)))
            diag_j = jnp.where(v < 4, v, jnp.where(w < 3, w + 1, jnp.where(w < 5, w - 1, 3)))
            i = jnp.where(me < 6, t // 8, jnp.where(diag, diag_i, half_i))
            j = jnp.where(me < 6, t % 8, jnp.where(diag, diag_j * 2 + t % 2, half_j))
            return i, j, jnp.logical_and(diag, v < 4)

        def place(t):
            i, j, same = tile(t)
            i0 = pl.multiple_of((i % 2) * ROWS, ROWS)
            j0 = pl.multiple_of((j % 4) * COLS, COLS)
            return i // 2, i0, j // 4, j0, same

        def distances(t, out):
            ib, i0, jb, j0, same = place(jnp.minimum(t, count - 1))
            out[...] = jnp.dot(
                amat[ib, pl.ds(i0, ROWS), :], pts[right + jb, :, pl.ds(j0, COLS)], preferred_element_type=f32
            )

        def products(t, dist):
            ib, i0, jb, j0, same = place(t)
            values = matern(dist[...])
            weight = jnp.where(same, 0.5, 1.0).astype(bf16)
            di = dmat[left + ib, :, pl.ds(i0, ROWS)] * weight
            dj = dmat[right + jb, :, pl.ds(j0, COLS)] * weight
            first[ph * 2 + ib, :, pl.ds(i0, ROWS)] += lax.dot_general(
                dj, values, (((1,), (1,)), ((), ())), preferred_element_type=f32
            )
            second[ph * 2 + jb, :, pl.ds(j0, COLS)] += jnp.dot(di, values, preferred_element_type=f32)

        distances(0, even)

        def step(n, carry):
            for m in range(2):
                t = n * 4 + m * 2
                distances(t + 1, odd)
                products(t, even)
                distances(t + 2, even)
                products(t + 1, odd)
            return carry

        lax.fori_loop(0, count // 4, step, 0)

        @pl.when(diag)
        def _():
            for y in range(2):
                pack(y, first[y] + second[y])

        @pl.when(jnp.logical_not(diag))
        def _():
            for y in range(2):
                pack(left + y, first[ph * 2 + y])
                pack(right + y, second[ph * 2 + y])

        @pl.when(ph == 0)
        def _():
            for s in (0, 1):
                if_slot(s, parts_out(s, True))

        @pl.when(ph == 1)
        def _():
            for s in (2, 3):
                parts_out(s, True)()

        return carry

    lax.fori_loop(0, jnp.where(me < 6, 1, 2), phase, 0)

    for copy in loads[3:]:
        copy.wait()
    residual = res_ref[...]

    total = jnp.zeros((16, 256), f32)
    for u in range(len(USES)):
        pltpu.make_async_copy(got.at[u], got.at[u], part_recv.at[u]).wait()
        total += got[u].astype(f32)
    product = jnp.concatenate([total[c * 4 : c * 4 + 4, :] for c in range(4)], axis=1)
    image = 3.0 * product + noise_ref[0] * direction

    stats = jnp.concatenate(
        [
            jnp.sum(a, axis=1, keepdims=True)
            for a in (residual * residual, direction * image, residual * image, image * image)
        ],
        axis=0,
    )
    row = lax.broadcasted_iota(jnp.int32, (16, 128), 0)
    lane = lax.broadcasted_iota(jnp.int32, (16, 128), 1)
    sums[blk] = jnp.sum(jnp.where(row == lane, stats, 0.0), axis=0, keepdims=True)
    copies = [
        remote(sums.at[blk], sums.at[blk], sum_send.at[m], sum_recv.at[blk], peers[m]) for m in range(31)
    ]
    for copy in copies:
        copy.start()
    for m in range(1, 32):
        k = (blk + m) % 32
        pltpu.make_async_copy(sums.at[k], sums.at[k], sum_recv.at[k]).wait()
    stats = jnp.sum(jnp.where(row == lane, jnp.sum(sums[...], axis=0), 0.0), axis=1, keepdims=True)
    rr, curv, cross, norm = stats[0:4], stats[4:8], stats[8:12], stats[12:16]
    alpha = rr / curv
    rr_new = jnp.maximum(rr - 2.0 * alpha * cross + alpha * alpha * norm, 0.0)
    new_res = residual - alpha * image
    out_sol[...] = sol_ref[...] + alpha * direction
    out_res[...] = new_res
    out_dir[...] = new_res + (rr_new / rr) * direction

    points_out(False)
    dirs_out(False)
    for s in range(4):
        if_slot(s, parts_out(s, False))
    for copy in copies:
        copy.wait_send()


def on_device(points, lengthscale, noise, solution, residual, direction):
    vmem = pl.BlockSpec(memory_space=pltpu.VMEM)
    hbm = pl.BlockSpec(memory_space=pltpu.HBM)
    dma = pltpu.SemaphoreType.DMA
    probes = direction.shape[0]
    return pl.pallas_call(
        kernel,
        out_shape=[jax.ShapeDtypeStruct(direction.shape, f32)] * 3,
        in_specs=[hbm] * 6,
        out_specs=[vmem] * 3,
        scratch_shapes=[
            pltpu.VMEM((32, BLOCK), f32),
            pltpu.VMEM((1, 32), f32),
            pltpu.SMEM((1,), f32),
            pltpu.VMEM((probes, BLOCK), f32),
            pltpu.VMEM((probes, BLOCK), f32),
            pltpu.VMEM((probes, BLOCK), f32),
            pltpu.VMEM((32, BLOCK), bf16),
            pltpu.VMEM((16, 256), bf16),
            pltpu.VMEM((8, 48, BLOCK), bf16),
            pltpu.VMEM((32, 16, 256), bf16),
            pltpu.VMEM((8, 16, BLOCK), bf16),
            pltpu.VMEM((2, BLOCK, 48), bf16),
            pltpu.VMEM((ROWS, COLS), f32),
            pltpu.VMEM((ROWS, COLS), f32),
            pltpu.VMEM((4, 16, BLOCK), f32),
            pltpu.VMEM((4, 16, BLOCK), f32),
            pltpu.VMEM((32, 16, 256), bf16),
            pltpu.VMEM((len(USES), 16, 256), bf16),
            pltpu.VMEM((32, 1, 128), f32),
            dma((6,)), dma((6,)), dma((8,)), dma((len(USES),)), dma((32,)), dma((32,)), dma((len(USES),)),
            dma((31,)), dma((32,)),
        ],
        compiler_params=pltpu.CompilerParams(
            collective_id=0, has_side_effects=True
        ),
        cost_estimate=pl.CostEstimate(flops=2**31, bytes_accessed=2**20, transcendentals=2**23),
    )(points, lengthscale.reshape(1, 32), noise, solution, residual, direction)


def solution(mesh):
    in_specs = (P(None, "blk"), P(), P(), P("rep", "blk"), P("rep", "blk"), P("rep", "blk"))
    out_specs = (P("rep", "blk"), P("rep", "blk"), P("rep", "blk"))
    return jax.shard_map(
        on_device, mesh=mesh, in_specs=in_specs, out_specs=out_specs, check_vma=False
    )
```

```python
import math

import jax
import jax.numpy as jnp
from jax import lax
from jax.experimental import pallas as pl
from jax.experimental.pallas import tpu as pltpu
from jax.sharding import PartitionSpec as P

MESH = pl.DeviceIdType.MESH
bf16 = jnp.bfloat16
f32 = jnp.float32
BLOCK = 1024
ROWS = 512
COLS = 256
SCALE = math.sqrt(5.0) / 3.0
SLOTS = (
    ((0, 0), (0, 1), None, None),
    ((0, 0), (1, 0), None, None),
    ((-1, 0), (0, 1), None, None),
    ((-1, 0), (0, -1), None, None),
    ((0, -1), (1, 1), None, None),
    ((-1, 0), (1, 1), None, None),
    ((0, 0), None, (-1, -1), (1, 1)),
    ((0, -1), (0, 1), (-1, 0), (1, 0)),
)
USES = tuple((m, s) + SLOTS[m][s] for m in range(8) for s in range(4) if SLOTS[m][s] is not None)


def use_of(m, s):
    for index, use in enumerate(USES):
        if use[:2] == (m, s):
            return index
    return 0


def matern(dist):
    dist = jnp.maximum(dist, 1e-30)
    root = dist * lax.rsqrt(dist)
    decay = jnp.exp2(root * (-3.0 / math.log(2.0)))
    return ((root + dist + 1.0 / 3.0) * decay).astype(bf16)


def pick(index, values):
    result = jnp.int32(values[0])
    for k in range(1, len(values)):
        if values[k] != values[0]:
            result = jnp.where(index == k, jnp.int32(values[k]), result)
    return result


def squares(points):
    wide = points.astype(f32)
    total = jnp.sum(wide * wide, axis=0, keepdims=True)
    high = total.astype(bf16).astype(f32)
    rest = total - high
    mid = rest.astype(bf16).astype(f32)
    return (high, mid, rest - mid)


def kernel(
    points_hbm, length_hbm, noise_hbm, sol_hbm, res_hbm, dir_hbm,
    out_sol, out_res, out_dir,
    points_ref, length_ref, noise_ref, sol_ref, res_ref, dir_ref,
    mine, mydir, pts, dirs, dmat, amat, even, odd, first, second, parts, got, sums,
    load, pts_send, pts_recv, dir_send, dir_recv, part_send, part_recv, sum_send, sum_recv,
):
    blk = lax.axis_index("blk")
    rep = lax.axis_index("rep")
    ylo = blk & 1
    col = blk >> 1
    x = col >> 2
    z = col & 3
    me = ylo * 4 + rep

    def column(dx, dz):
        return ((x + dx + 4) & 3) * 4 + ((z + dz + 4) & 3)

    def member(c, k):
        return (c * 2 + (k >> 2), k & 3)

    def slot_column(s):
        offsets = [SLOTS[m][s] or (0, 0) for m in range(8)]
        return column(pick(me, [d[0] for d in offsets]), pick(me, [d[1] for d in offsets]))

    slot_cols = [slot_column(s) for s in range(4)]
    slot_use = [pick(me, [use_of(m, s) for m in range(8)]) for s in range(4)]
    own_pair = jnp.logical_or(jnp.logical_or(me == 0, me == 1), me == 6)
    users = [member(column(-dx, -dz), m) for m, s, dx, dz in USES]
    peers = [((blk + m) & 31, rep) for m in range(1, 32)]

    barrier = pltpu.get_barrier_semaphore()

    def hail(device):
        pl.semaphore_signal(barrier, inc=1, device_id=device, device_id_type=MESH)

    def if_slot(s, action):
        if s == 0:
            action()
        elif s == 1:
            pl.when(me != 6)(action)
        else:
            pl.when(me >= 6)(action)

    def hail_sources(s):
        def action():
            for m in range(1, 8):
                hail(member(slot_cols[s], (me + m) & 7))
            if s == 0:
                pl.when(jnp.logical_not(own_pair))(lambda: hail(member(slot_cols[s], me)))
            else:
                hail(member(slot_cols[s], me))
        return action

    for s in range(4):
        if_slot(s, hail_sources(s))
    loads = [
        pltpu.make_async_copy(a, b, load.at[n])
        for n, (a, b) in enumerate(
            [
                (points_hbm, points_ref), (length_hbm, length_ref), (dir_hbm, dir_ref),
                (noise_hbm, noise_ref), (sol_hbm, sol_ref), (res_hbm, res_ref),
            ]
        )
    ]
    for copy in loads:
        copy.start()


    for copy in loads[:3]:
        copy.wait()
    row = lax.broadcasted_iota(jnp.int32, (32, 32), 0)
    lane = lax.broadcasted_iota(jnp.int32, (32, 32), 1)
    length = jnp.sum(jnp.where(row == lane, length_ref[...], 0.0), axis=1, keepdims=True)
    mine[...] = (points_ref[...] * (SCALE / length)).astype(bf16)
    direction = dir_ref[...]
    mydir[...] = jnp.concatenate(
        [direction[:, c * 256 : (c + 1) * 256] for c in range(4)], axis=0
    ).astype(bf16)

    pl.semaphore_wait(barrier, len(USES) - jnp.where(own_pair, 1, 0))

    def remote(src, dst, send_sem, recv_sem, device):
        return pltpu.make_async_remote_copy(
            src_ref=src, dst_ref=dst, send_sem=send_sem, recv_sem=recv_sem,
            device_id=device, device_id_type=MESH,
        )

    def deliver(src, dst, send_sem, recv_sem, device, is_self):
        def away():
            remote(src, dst, send_sem, recv_sem, device).start()

        if is_self is None:
            away()
        else:
            pl.when(is_self)(lambda: pltpu.make_async_copy(src, dst, recv_sem).start())
            pl.when(jnp.logical_not(is_self))(away)

    def drain(ref, sem):
        pltpu.make_async_copy(ref, ref, sem).wait()

    def drain_either(alone, ref, count, sem):
        pl.when(alone)(lambda: drain(ref.at[pl.ds(0, count - 1)], sem))
        pl.when(jnp.logical_not(alone))(lambda: drain(ref.at[pl.ds(0, count)], sem))

    for u, (m, s, dx, dz) in enumerate(USES):
        deliver(
            mydir, dirs.at[s * 8 + me], dir_send.at[0], dir_recv.at[s], users[u],
            me == m if (dx, dz) == (0, 0) else None,
        )

    def points_out(r):
        def action():
            for u, (m, s, dx, dz) in enumerate(USES):
                if m % 4 == r:
                    place = s * 2 + ylo
                    deliver(
                        mine, pts.at[place, pl.ds(0, 32)], pts_send.at[0], pts_recv.at[place], users[u],
                        me == m if (dx, dz) == (0, 0) else None,
                    )
        return action

    for r in range(4):
        pl.when(rep == r)(points_out(r))
    first[...] = jnp.zeros_like(first)
    second[...] = jnp.zeros_like(second)

    def augment(place):
        drain(pts.at[place, pl.ds(0, 32)], pts_recv.at[place])
        high, mid, low = squares(pts[place, 0:32, :])
        one = jnp.ones((1, BLOCK), f32)
        extra = jnp.concatenate([high, mid, low, one, one, one, jnp.zeros((10, BLOCK), f32)], axis=0)
        pts[place, 32:48, :] = extra.astype(bf16)

    def left_rows(place, y):
        q = pts[place, 0:32, :]
        high, mid, low = squares(q)
        one = jnp.ones((1, BLOCK), f32)
        whole = jnp.concatenate(
            [q.astype(f32) * -2.0, one, one, one, high, mid, low, jnp.zeros((10, BLOCK), f32)], axis=0
        )
        amat[y] = jnp.transpose(whole).astype(bf16)

    def spread(place):
        pieces = []
        for r in range(4):
            k = place * 4 + r
            pieces.append(dirs[k].astype(f32))
        for c in range(4):
            rows = jnp.concatenate([p[c * 4 : c * 4 + 4, :] for p in pieces], axis=0)
            dmat[place, :, c * 256 : (c + 1) * 256] = rows.astype(bf16)

    def pack(place, whole):
        for r in range(4):
            piece = [whole[r * 4 : r * 4 + 4, c * 256 : (c + 1) * 256] for c in range(4)]
            parts[place * 4 + r] = jnp.concatenate(piece, axis=0).astype(bf16)

    def parts_out(s):
        def action():
            for m in range(8):
                k = (me + m) & 7
                deliver(
                    parts.at[s * 8 + k], got.at[slot_use[s]], part_send.at[s], part_recv.at[0],
                    member(slot_cols[s], k), own_pair if s == 0 and m == 0 else None,
                )
        return action

    def phase(ph, carry):
        diag = jnp.logical_and(me == 6, ph == 0)
        left = ph * 4
        right = jnp.where(diag, 0, ph * 4 + 2)
        for y in range(2):
            augment(left + y)
            left_rows(left + y, y)

        @pl.when(jnp.logical_not(diag))
        def _():
            for y in range(2):
                augment(right + y)

        drain(dirs.at[pl.ds(left * 4, 8)], dir_recv.at[ph * 2])
        for y in range(2):
            spread(left + y)

        @pl.when(jnp.logical_not(diag))
        def _():
            drain(dirs.at[pl.ds(right * 4, 8)], dir_recv.at[ph * 2 + 1])
            for y in range(2):
                spread(right + y)

        low_col = jnp.where(ph == 0, slot_cols[0], slot_cols[2])
        high_col = jnp.where(ph == 0, slot_cols[1], slot_cols[3])
        early = jnp.where(low_col < high_col, 0, 1)
        count = jnp.where(me < 6, 32, jnp.where(diag, 20, 16))

        def tile(t):
            u = t - 8
            half_i = jnp.where(t < 8, t >> 2, 2 * early + (u >> 2))
            half_j = jnp.where(t < 8, 4 + (t & 3), 4 * early + (t & 3))
            v = t >> 1
            w = v - 4
            diag_i = jnp.where(v < 4, v, jnp.where(w < 3, 0, jnp.where(w < 5, 1, 2)))
            diag_j = jnp.where(v < 4, v, jnp.where(w < 3, w + 1, jnp.where(w < 5, w - 1, 3)))
            i = jnp.where(me < 6, t >> 3, jnp.where(diag, diag_i, half_i))
            j = jnp.where(me < 6, t & 7, jnp.where(diag, diag_j * 2 + (t & 1), half_j))
            return i, j, jnp.logical_and(diag, v < 4)

        def place(t):
            i, j, same = tile(t)
            i0 = pl.multiple_of((i & 1) * ROWS, ROWS)
            j0 = pl.multiple_of((j & 3) * COLS, COLS)
            return i >> 1, i0, j >> 2, j0, same

        def distances(t, out):
            ib, i0, jb, j0, same = place(jnp.minimum(t, count - 1))
            out[...] = jnp.dot(
                amat[ib, pl.ds(i0, ROWS), :], pts[right + jb, :, pl.ds(j0, COLS)], preferred_element_type=f32
            )

        def products(t, dist):
            ib, i0, jb, j0, same = place(t)
            values = matern(dist[...])
            weight = jnp.where(same, 0.5, 1.0).astype(bf16)
            di = dmat[left + ib, :, pl.ds(i0, ROWS)] * weight
            dj = dmat[right + jb, :, pl.ds(j0, COLS)] * weight
            first[ph * 2 + ib, :, pl.ds(i0, ROWS)] += lax.dot_general(
                dj, values, (((1,), (1,)), ((), ())), preferred_element_type=f32
            )
            second[ph * 2 + jb, :, pl.ds(j0, COLS)] += jnp.dot(di, values, preferred_element_type=f32)

        distances(0, even)

        def step(n, carry):
            for m in range(2):
                t = n * 4 + m * 2
                distances(t + 1, odd)
                products(t, even)
                distances(t + 2, even)
                products(t + 1, odd)
            return carry

        lax.fori_loop(0, count >> 2, step, 0)

        @pl.when(diag)
        def _():
            for y in range(2):
                pack(y, first[y] + second[y])

        @pl.when(jnp.logical_not(diag))
        def _():
            for y in range(2):
                pack(left + y, first[ph * 2 + y])
                pack(right + y, second[ph * 2 + y])

        @pl.when(ph == 0)
        def _():
            for s in (0, 1):
                if_slot(s, parts_out(s))

        @pl.when(ph == 1)
        def _():
            for s in (2, 3):
                parts_out(s)()

        return carry

    lax.fori_loop(0, jnp.where(me < 6, 1, 2), phase, 0)

    for copy in loads[3:]:
        copy.wait()
    residual = res_ref[...]

    total = jnp.zeros((16, 256), f32)
    drain(got, part_recv.at[0])
    for u in range(len(USES)):
        total += got[u].astype(f32)
    product = jnp.concatenate([total[c * 4 : c * 4 + 4, :] for c in range(4)], axis=1)
    image = 3.0 * product + noise_ref[0] * direction

    stats = jnp.concatenate(
        [
            jnp.sum(a, axis=1, keepdims=True)
            for a in (residual * residual, direction * image, residual * image, image * image)
        ],
        axis=0,
    )
    row = lax.broadcasted_iota(jnp.int32, (16, 128), 0)
    lane = lax.broadcasted_iota(jnp.int32, (16, 128), 1)
    sums[blk] = jnp.sum(jnp.where(row == lane, stats, 0.0), axis=0, keepdims=True)
    copies = [
        remote(sums.at[blk], sums.at[blk], sum_send.at[0], sum_recv.at[0], peers[m]) for m in range(31)
    ]
    for copy in copies:
        copy.start()
    drain(sums.at[pl.ds(0, 31)], sum_recv.at[0])
    stats = jnp.sum(jnp.where(row == lane, jnp.sum(sums[...], axis=0), 0.0), axis=1, keepdims=True)
    rr, curv, cross, norm = stats[0:4], stats[4:8], stats[8:12], stats[12:16]
    alpha = rr / curv
    rr_new = jnp.maximum(rr - 2.0 * alpha * cross + alpha * alpha * norm, 0.0)
    new_res = residual - alpha * image
    out_sol[...] = sol_ref[...] + alpha * direction
    out_res[...] = new_res
    out_dir[...] = new_res + (rr_new / rr) * direction

    drain_either(own_pair, dirs, len(USES), dir_send.at[0])
    for r in range(4):
        count = sum(m % 4 == r for m, *_ in USES)

        @pl.when(rep == r)
        def _():
            drain_either(own_pair, pts.at[:, pl.ds(0, 32)], count, pts_send.at[0])

    for s in range(4):
        if s == 0:
            drain_either(own_pair, parts, 8, part_send.at[s])
        else:
            if_slot(s, lambda: drain(parts.at[pl.ds(0, 8)], part_send.at[s]))
    drain(sums.at[pl.ds(0, 31)], sum_send.at[0])


def store(a, b, c, out_a, out_b, out_c, sem):
    copies = [
        pltpu.make_async_copy(src, dst, sem.at[n])
        for n, (src, dst) in enumerate([(a, out_a), (b, out_b), (c, out_c)])
    ]
    for copy in copies:
        copy.start()
    for copy in copies:
        copy.wait()


def on_device(points, lengthscale, noise, solution, residual, direction):
    vmem = pl.BlockSpec(memory_space=pltpu.VMEM)
    hbm = pl.BlockSpec(memory_space=pltpu.HBM)
    dma = pltpu.SemaphoreType.DMA
    probes = direction.shape[0]
    results = pl.pallas_call(
        kernel,
        out_shape=[jax.ShapeDtypeStruct(direction.shape, f32)] * 3,
        in_specs=[hbm] * 6,
        out_specs=[vmem] * 3,
        scratch_shapes=[
            pltpu.VMEM((32, BLOCK), f32),
            pltpu.VMEM((1, 32), f32),
            pltpu.SMEM((1,), f32),
            pltpu.VMEM((probes, BLOCK), f32),
            pltpu.VMEM((probes, BLOCK), f32),
            pltpu.VMEM((probes, BLOCK), f32),
            pltpu.VMEM((32, BLOCK), bf16),
            pltpu.VMEM((16, 256), bf16),
            pltpu.VMEM((8, 48, BLOCK), bf16),
            pltpu.VMEM((32, 16, 256), bf16),
            pltpu.VMEM((8, 16, BLOCK), bf16),
            pltpu.VMEM((2, BLOCK, 48), bf16),
            pltpu.VMEM((ROWS, COLS), f32),
            pltpu.VMEM((ROWS, COLS), f32),
            pltpu.VMEM((4, 16, BLOCK), f32),
            pltpu.VMEM((4, 16, BLOCK), f32),
            pltpu.VMEM((32, 16, 256), bf16),
            pltpu.VMEM((len(USES), 16, 256), bf16),
            pltpu.VMEM((32, 1, 128), f32),
            dma((6,)), dma((1,)), dma((8,)), dma((1,)), dma((4,)), dma((4,)), dma((1,)), dma((1,)), dma((1,)),
        ],
        compiler_params=pltpu.CompilerParams(
            collective_id=0, has_side_effects=True
        ),
        cost_estimate=pl.CostEstimate(flops=2**31, bytes_accessed=2**20, transcendentals=2**23),
    )(points, lengthscale.reshape(1, 32), noise, solution, residual, direction)
    return pl.pallas_call(
        store,
        out_shape=[jax.ShapeDtypeStruct(direction.shape, f32)] * 3,
        in_specs=[vmem] * 3,
        out_specs=[hbm] * 3,
        scratch_shapes=[dma((3,))],
    )(*results)


def solution(mesh):
    in_specs = (P(None, "blk"), P(), P(), P("rep", "blk"), P("rep", "blk"), P("rep", "blk"))
    out_specs = (P("rep", "blk"), P("rep", "blk"), P("rep", "blk"))
    return jax.shard_map(
        on_device, mesh=mesh, in_specs=in_specs, out_specs=out_specs, check_vma=False
    )
```

```python
import math

import jax
import jax.numpy as jnp
from jax import lax
from jax.experimental import pallas as pl
from jax.experimental.pallas import tpu as pltpu
from jax.sharding import PartitionSpec as P

MESH = pl.DeviceIdType.MESH
bf16 = jnp.bfloat16
f32 = jnp.float32
BLOCK = 1024
ROWS = 512
COLS = 256
SCALE = math.sqrt(5.0) / 3.0
SLOTS = (
    ((0, -1), (1, 1), None, None),
    ((-1, 0), (1, 1), None, None),
    ((0, 0), (0, 1), None, None),
    ((0, 0), (1, 0), None, None),
    ((0, 0), None, (-1, -1), (1, 1)),
    ((-1, 0), (0, 1), None, None),
    ((-1, 0), (0, -1), None, None),
    ((0, -1), (0, 1), (-1, 0), (1, 0)),
)
DIAG = 4
HALVES = 7
USES = tuple((m, s) + SLOTS[m][s] for m in range(8) for s in range(4) if SLOTS[m][s] is not None)


def use_of(m, s):
    for index, use in enumerate(USES):
        if use[:2] == (m, s):
            return index
    return 0


def matern(dist):
    dist = jnp.maximum(dist, 1e-30)
    root = dist * lax.rsqrt(dist)
    decay = jnp.exp2(root * (-3.0 / math.log(2.0)))
    return ((root + dist + 1.0 / 3.0) * decay).astype(bf16)


def pick(index, values):
    result = jnp.int32(values[0])
    for k in range(1, len(values)):
        if values[k] != values[0]:
            result = jnp.where(index == k, jnp.int32(values[k]), result)
    return result


def squares(points):
    wide = points.astype(f32)
    total = jnp.sum(wide * wide, axis=0, keepdims=True)
    high = total.astype(bf16).astype(f32)
    rest = total - high
    mid = rest.astype(bf16).astype(f32)
    return (high, mid, rest - mid)


def kernel(
    points_hbm, length_hbm, noise_hbm, sol_hbm, res_hbm, dir_hbm,
    out_sol, out_res, out_dir,
    points_ref, length_ref, noise_ref, sol_ref, res_ref, dir_ref,
    mine, mydir, pts, dirs, dmat, amat, even, odd, first, second, parts, got, sums,
    load, pts_send, pts_recv, dir_send, dir_recv, part_send, part_recv, sum_send, sum_recv,
):
    blk = lax.axis_index("blk")
    rep = lax.axis_index("rep")
    ylo = blk & 1
    col = blk >> 1
    x = col >> 2
    z = col & 3
    me = ylo * 4 + rep

    def column(dx, dz):
        return ((x + dx + 4) & 3) * 4 + ((z + dz + 4) & 3)

    def member(c, k):
        return (c * 2 + (k >> 2), k & 3)

    def slot_column(s):
        offsets = [SLOTS[m][s] or (0, 0) for m in range(8)]
        return column(pick(me, [d[0] for d in offsets]), pick(me, [d[1] for d in offsets]))

    slot_cols = [slot_column(s) for s in range(4)]
    slot_use = [pick(me, [use_of(m, s) for m in range(8)]) for s in range(4)]
    own_pair = jnp.logical_or(jnp.logical_or(me == 2, me == 3), me == DIAG)
    two = jnp.logical_or(me == DIAG, me == HALVES)
    users = [member(column(-dx, -dz), m) for m, s, dx, dz in USES]
    peers = [((blk + m) & 31, rep) for m in range(1, 32)]

    barrier = pltpu.get_barrier_semaphore()

    def hail(device):
        pl.semaphore_signal(barrier, inc=1, device_id=device, device_id_type=MESH)

    def if_slot(s, action):
        if s == 0:
            action()
        elif s == 1:
            pl.when(me != DIAG)(action)
        else:
            pl.when(two)(action)

    def hail_sources(s):
        def action():
            for m in range(1, 8):
                hail(member(slot_cols[s], (me + m) & 7))
            if s == 0:
                pl.when(jnp.logical_not(own_pair))(lambda: hail(member(slot_cols[s], me)))
            else:
                hail(member(slot_cols[s], me))
        return action

    for s in range(4):
        if_slot(s, hail_sources(s))
    loads = [
        pltpu.make_async_copy(a, b, load.at[n])
        for n, (a, b) in enumerate(
            [
                (points_hbm, points_ref), (length_hbm, length_ref), (dir_hbm, dir_ref),
                (noise_hbm, noise_ref), (sol_hbm, sol_ref), (res_hbm, res_ref),
            ]
        )
    ]
    for copy in loads:
        copy.start()


    for copy in loads[:3]:
        copy.wait()
    row = lax.broadcasted_iota(jnp.int32, (32, 32), 0)
    lane = lax.broadcasted_iota(jnp.int32, (32, 32), 1)
    length = jnp.sum(jnp.where(row == lane, length_ref[...], 0.0), axis=1, keepdims=True)
    mine[...] = (points_ref[...] * (SCALE / length)).astype(bf16)
    direction = dir_ref[...]
    mydir[...] = jnp.concatenate(
        [direction[:, c * 256 : (c + 1) * 256] for c in range(4)], axis=0
    ).astype(bf16)

    pl.semaphore_wait(barrier, len(USES) - jnp.where(own_pair, 1, 0))

    def remote(src, dst, send_sem, recv_sem, device):
        return pltpu.make_async_remote_copy(
            src_ref=src, dst_ref=dst, send_sem=send_sem, recv_sem=recv_sem,
            device_id=device, device_id_type=MESH,
        )

    def deliver(src, dst, send_sem, recv_sem, device, is_self):
        def away():
            remote(src, dst, send_sem, recv_sem, device).start()

        if is_self is None:
            away()
        else:
            pl.when(is_self)(lambda: pltpu.make_async_copy(src, dst, recv_sem).start())
            pl.when(jnp.logical_not(is_self))(away)

    def drain(ref, sem):
        pltpu.make_async_copy(ref, ref, sem).wait()

    def drain_either(alone, ref, count, sem):
        pl.when(alone)(lambda: drain(ref.at[pl.ds(0, count - 1)], sem))
        pl.when(jnp.logical_not(alone))(lambda: drain(ref.at[pl.ds(0, count)], sem))

    for u, (m, s, dx, dz) in enumerate(USES):
        deliver(
            mydir, dirs.at[s * 8 + me], dir_send.at[0], dir_recv.at[s * 2 + ylo], users[u],
            me == m if (dx, dz) == (0, 0) else None,
        )

    def points_out(r):
        def action():
            for u, (m, s, dx, dz) in enumerate(USES):
                if m % 4 == r:
                    place = s * 2 + ylo
                    deliver(
                        mine, pts.at[place, pl.ds(0, 32)], pts_send.at[0], pts_recv.at[place], users[u],
                        me == m if (dx, dz) == (0, 0) else None,
                    )
        return action

    for r in range(4):
        pl.when(rep == r)(points_out(r))
    first[...] = jnp.zeros_like(first)
    second[...] = jnp.zeros_like(second)

    def augment(place):
        drain(pts.at[place, pl.ds(0, 32)], pts_recv.at[place])
        high, mid, low = squares(pts[place, 0:32, :])
        one = jnp.ones((1, BLOCK), f32)
        extra = jnp.concatenate([high, mid, low, one, one, one, jnp.zeros((10, BLOCK), f32)], axis=0)
        pts[place, 32:48, :] = extra.astype(bf16)

    def left_rows(place, y):
        q = pts[place, 0:32, :]
        high, mid, low = squares(q)
        one = jnp.ones((1, BLOCK), f32)
        whole = jnp.concatenate(
            [q.astype(f32) * -2.0, one, one, one, high, mid, low, jnp.zeros((10, BLOCK), f32)], axis=0
        )
        amat[y] = jnp.transpose(whole).astype(bf16)

    def spread(place):
        drain(dirs.at[pl.ds(place * 4, 4)], dir_recv.at[place])
        pieces = [dirs[place * 4 + r].astype(f32) for r in range(4)]
        for c in range(4):
            rows = jnp.concatenate([p[c * 4 : c * 4 + 4, :] for p in pieces], axis=0)
            dmat[place, :, c * 256 : (c + 1) * 256] = rows.astype(bf16)

    def pack(place, whole):
        for r in range(4):
            piece = [whole[r * 4 : r * 4 + 4, c * 256 : (c + 1) * 256] for c in range(4)]
            parts[place * 4 + r] = jnp.concatenate(piece, axis=0).astype(bf16)

    def parts_out(s, y):
        def action():
            for m in range(4):
                r = (me + m) & 3
                deliver(
                    parts.at[s * 8 + y * 4 + r], got.at[slot_use[s]], part_send.at[s], part_recv.at[0],
                    member(slot_cols[s], y * 4 + r),
                    jnp.logical_and(own_pair, ylo == y) if s == 0 and m == 0 else None,
                )
        return action

    def phase(ph, carry):
        diag = jnp.logical_and(me == DIAG, ph == 0)
        left = ph * 4
        right = jnp.where(diag, 0, ph * 4 + 2)
        for y in range(2):
            augment(left + y)
            left_rows(left + y, y)

        @pl.when(jnp.logical_not(diag))
        def _():
            for y in range(2):
                augment(right + y)

        def spread_pair(b):
            spread(left + b)

            @pl.when(jnp.logical_not(diag))
            def _():
                spread(right + b)

        near = 1 - ylo
        spread_pair(near)

        low_col = jnp.where(ph == 0, slot_cols[0], slot_cols[2])
        high_col = jnp.where(ph == 0, slot_cols[1], slot_cols[3])
        early = jnp.where(low_col < high_col, 0, 1)
        full = jnp.logical_not(two)
        count = jnp.where(full, 32, jnp.where(diag, 20, 16))

        def tile(t):
            u = t - 8
            half_i = jnp.where(t < 8, t >> 2, 2 * early + (u >> 2))
            half_j = jnp.where(t < 8, 4 + (t & 3), 4 * early + (t & 3))
            v = t >> 1
            w = v - 4
            diag_i = jnp.where(v < 4, v, jnp.where(w < 3, 0, jnp.where(w < 5, 1, 2)))
            diag_j = jnp.where(v < 4, v, jnp.where(w < 3, w + 1, jnp.where(w < 5, w - 1, 3)))
            i = jnp.where(full, 2 * ((t >> 4) ^ near) + ((t >> 2) & 1), jnp.where(diag, diag_i, half_i))
            j = jnp.where(full, 4 * (((t >> 3) & 1) ^ near) + (t & 3), jnp.where(diag, diag_j * 2 + (t & 1), half_j))
            return i, j, jnp.logical_and(diag, v < 4)

        def place(t):
            i, j, same = tile(t)
            i0 = pl.multiple_of((i & 1) * ROWS, ROWS)
            j0 = pl.multiple_of((j & 3) * COLS, COLS)
            return i >> 1, i0, j >> 2, j0, same

        def distances(t, out):
            ib, i0, jb, j0, same = place(jnp.minimum(t, count - 1))
            out[...] = jnp.dot(
                amat[ib, pl.ds(i0, ROWS), :], pts[right + jb, :, pl.ds(j0, COLS)], preferred_element_type=f32
            )

        def products(t, dist):
            ib, i0, jb, j0, same = place(t)
            values = matern(dist[...])
            weight = jnp.where(same, 0.5, 1.0).astype(bf16)
            di = dmat[left + ib, :, pl.ds(i0, ROWS)] * weight
            dj = dmat[right + jb, :, pl.ds(j0, COLS)] * weight
            first[ph * 2 + ib, :, pl.ds(i0, ROWS)] += lax.dot_general(
                dj, values, (((1,), (1,)), ((), ())), preferred_element_type=f32
            )
            second[ph * 2 + jb, :, pl.ds(j0, COLS)] += jnp.dot(di, values, preferred_element_type=f32)

        distances(0, even)

        def step(n, carry):
            for m in range(2):
                t = n * 4 + m * 2
                distances(t + 1, odd)
                products(t, even)
                distances(t + 2, even)
                products(t + 1, odd)
            return carry

        def finish(side, b):
            slot = ph * 2 + side
            whole = (first, second)[side][ph * 2 + b]
            if side == 0:
                whole = jnp.where(diag, whole + second[ph * 2 + b], whole)
            pack(slot * 2 + b, whole)
            for s in (side, 2 + side):
                pl.when(ph * 2 + side == s)(parts_out(s, b))

        def segment(q, carry):
            begin = jnp.where(full, 2 * q, 0)
            end = jnp.where(full, 2 * q + 2, jnp.where(q == 1, count >> 2, 0))
            lax.fori_loop(begin, end, step, 0)

            @pl.when(q == 0)
            def _():
                spread_pair(ylo)

            @pl.when(jnp.logical_and(full, q == 1))
            def _():
                finish(0, near)

            @pl.when(jnp.logical_and(full, q == 2))
            def _():
                finish(1, near)

            return carry

        lax.fori_loop(0, 4, segment, 0)
        finish(0, ylo)

        @pl.when(jnp.logical_not(diag))
        def _():
            finish(1, ylo)

        @pl.when(two)
        def _():
            finish(0, near)

        @pl.when(jnp.logical_and(two, jnp.logical_not(diag)))
        def _():
            finish(1, near)

        return carry

    lax.fori_loop(0, jnp.where(two, 2, 1), phase, 0)

    for copy in loads[3:]:
        copy.wait()
    residual = res_ref[...]

    total = jnp.zeros((16, 256), f32)
    drain(got, part_recv.at[0])
    for u in range(len(USES)):
        total += got[u].astype(f32)
    product = jnp.concatenate([total[c * 4 : c * 4 + 4, :] for c in range(4)], axis=1)
    image = 3.0 * product + noise_ref[0] * direction

    stats = jnp.concatenate(
        [
            jnp.sum(a, axis=1, keepdims=True)
            for a in (residual * residual, direction * image, residual * image, image * image)
        ],
        axis=0,
    )
    row = lax.broadcasted_iota(jnp.int32, (16, 128), 0)
    lane = lax.broadcasted_iota(jnp.int32, (16, 128), 1)
    sums[blk] = jnp.sum(jnp.where(row == lane, stats, 0.0), axis=0, keepdims=True)
    copies = [
        remote(sums.at[blk], sums.at[blk], sum_send.at[0], sum_recv.at[0], peers[m]) for m in range(31)
    ]
    for copy in copies:
        copy.start()
    drain(sums.at[pl.ds(0, 31)], sum_recv.at[0])
    stats = jnp.sum(jnp.where(row == lane, jnp.sum(sums[...], axis=0), 0.0), axis=1, keepdims=True)
    rr, curv, cross, norm = stats[0:4], stats[4:8], stats[8:12], stats[12:16]
    alpha = rr / curv
    rr_new = jnp.maximum(rr - 2.0 * alpha * cross + alpha * alpha * norm, 0.0)
    new_res = residual - alpha * image
    out_sol[...] = sol_ref[...] + alpha * direction
    out_res[...] = new_res
    out_dir[...] = new_res + (rr_new / rr) * direction

    drain_either(own_pair, dirs, len(USES), dir_send.at[0])
    for r in range(4):
        count = sum(m % 4 == r for m, *_ in USES)

        @pl.when(rep == r)
        def _():
            drain_either(own_pair, pts.at[:, pl.ds(0, 32)], count, pts_send.at[0])

    for s in range(4):
        if s == 0:
            drain_either(own_pair, parts, 8, part_send.at[s])
        else:
            if_slot(s, lambda: drain(parts.at[pl.ds(0, 8)], part_send.at[s]))
    drain(sums.at[pl.ds(0, 31)], sum_send.at[0])


def store(a, b, c, out_a, out_b, out_c, sem):
    copies = [
        pltpu.make_async_copy(src, dst, sem.at[n])
        for n, (src, dst) in enumerate([(a, out_a), (b, out_b), (c, out_c)])
    ]
    for copy in copies:
        copy.start()
    for copy in copies:
        copy.wait()


def on_device(points, lengthscale, noise, solution, residual, direction):
    vmem = pl.BlockSpec(memory_space=pltpu.VMEM)
    hbm = pl.BlockSpec(memory_space=pltpu.HBM)
    dma = pltpu.SemaphoreType.DMA
    probes = direction.shape[0]
    results = pl.pallas_call(
        kernel,
        out_shape=[jax.ShapeDtypeStruct(direction.shape, f32)] * 3,
        in_specs=[hbm] * 6,
        out_specs=[vmem] * 3,
        scratch_shapes=[
            pltpu.VMEM((32, BLOCK), f32),
            pltpu.VMEM((1, 32), f32),
            pltpu.SMEM((1,), f32),
            pltpu.VMEM((probes, BLOCK), f32),
            pltpu.VMEM((probes, BLOCK), f32),
            pltpu.VMEM((probes, BLOCK), f32),
            pltpu.VMEM((32, BLOCK), bf16),
            pltpu.VMEM((16, 256), bf16),
            pltpu.VMEM((8, 48, BLOCK), bf16),
            pltpu.VMEM((32, 16, 256), bf16),
            pltpu.VMEM((8, 16, BLOCK), bf16),
            pltpu.VMEM((2, BLOCK, 48), bf16),
            pltpu.VMEM((ROWS, COLS), f32),
            pltpu.VMEM((ROWS, COLS), f32),
            pltpu.VMEM((4, 16, BLOCK), f32),
            pltpu.VMEM((4, 16, BLOCK), f32),
            pltpu.VMEM((32, 16, 256), bf16),
            pltpu.VMEM((len(USES), 16, 256), bf16),
            pltpu.VMEM((32, 1, 128), f32),
            dma((6,)), dma((1,)), dma((8,)), dma((1,)), dma((8,)), dma((4,)), dma((1,)), dma((1,)), dma((1,)),
        ],
        compiler_params=pltpu.CompilerParams(
            collective_id=0, has_side_effects=True
        ),
        cost_estimate=pl.CostEstimate(flops=2**31, bytes_accessed=2**20, transcendentals=2**23),
    )(points, lengthscale.reshape(1, 32), noise, solution, residual, direction)
    return pl.pallas_call(
        store,
        out_shape=[jax.ShapeDtypeStruct(direction.shape, f32)] * 3,
        in_specs=[vmem] * 3,
        out_specs=[hbm] * 3,
        scratch_shapes=[dma((3,))],
    )(*results)


def solution(mesh):
    in_specs = (P(None, "blk"), P(), P(), P("rep", "blk"), P("rep", "blk"), P("rep", "blk"))
    out_specs = (P("rep", "blk"), P("rep", "blk"), P("rep", "blk"))
    return jax.shard_map(
        on_device, mesh=mesh, in_specs=in_specs, out_specs=out_specs, check_vma=False
    )
```

```python
import math

import jax
import jax.numpy as jnp
from jax import lax
from jax.experimental import pallas as pl
from jax.experimental.pallas import tpu as pltpu
from jax.sharding import PartitionSpec as P

MESH = pl.DeviceIdType.MESH
bf16 = jnp.bfloat16
f32 = jnp.float32
BLOCK = 1024
ROWS = 512
COLS = 256
SCALE = math.sqrt(5.0) / 3.0
SLOTS = (
    ((-1, -1), (1, 1), (-1, 0), (1, 0)),
    ((0, 0), (0, 1), None, None),
    ((0, 0), (1, 0), None, None),
    ((-1, 0), (0, 1), None, None),
    ((0, -1), (1, 1), None, None),
    ((-1, 0), (1, 1), None, None),
    ((-1, 0), (0, -1), None, None),
    ((0, -1), (0, 1), (-1, 0), (1, 0)),
)
OWN = (1, 2)
HALVES = (0, 7)
USES = tuple((m, s) + SLOTS[m][s] for m in range(8) for s in range(4) if SLOTS[m][s] is not None)
URGENT = sorted(range(len(USES)), key=lambda u: (USES[u][1] > 1, -abs(USES[u][2]) - abs(USES[u][3])))


def use_of(m, s):
    for index, use in enumerate(USES):
        if use[:2] == (m, s):
            return index
    return 0


def matern(dist):
    dist = jnp.maximum(dist, 1e-30)
    root = dist * lax.rsqrt(dist)
    decay = jnp.exp2(root * (-3.0 / math.log(2.0)))
    return ((root + dist + 1.0 / 3.0) * decay).astype(bf16)


def pick(index, values):
    result = jnp.int32(values[0])
    for k in range(1, len(values)):
        if values[k] != values[0]:
            result = jnp.where(index == k, jnp.int32(values[k]), result)
    return result


def squares(points):
    wide = points.astype(f32)
    total = jnp.sum(wide * wide, axis=0, keepdims=True)
    high = total.astype(bf16).astype(f32)
    rest = total - high
    mid = rest.astype(bf16).astype(f32)
    return (high, mid, rest - mid)


def kernel(
    points_hbm, length_hbm, noise_hbm, sol_hbm, res_hbm, dir_hbm,
    out_sol, out_res, out_dir,
    points_ref, length_ref, noise_ref, sol_ref, res_ref, dir_ref,
    mine, mydir, pts, dirs, dmat, amat, even, odd, first, second, parts, got, sums,
    load, pts_send, pts_recv, dir_send, dir_recv, part_send, part_recv, sum_send, sum_recv,
):
    blk = lax.axis_index("blk")
    rep = lax.axis_index("rep")
    ylo = blk & 1
    col = blk >> 1
    x = col >> 2
    z = col & 3
    me = ylo * 4 + rep

    def column(dx, dz):
        return ((x + dx + 4) & 3) * 4 + ((z + dz + 4) & 3)

    def member(c, k):
        return (c * 2 + (k >> 2), k & 3)

    def slot_column(s):
        offsets = [SLOTS[m][s] or (0, 0) for m in range(8)]
        return column(pick(me, [d[0] for d in offsets]), pick(me, [d[1] for d in offsets]))

    slot_cols = [slot_column(s) for s in range(4)]
    slot_use = [pick(me, [use_of(m, s) for m in range(8)]) for s in range(4)]
    own_pair = jnp.logical_or(me == OWN[0], me == OWN[1])
    halves = jnp.logical_or(me == HALVES[0], me == HALVES[1])
    users = [member(column(-dx, -dz), m) for m, s, dx, dz in USES]
    hops = (0, 1, 2, 1)
    masks = sorted(range(1, 32), key=lambda m: -(hops[m >> 3] + hops[(m >> 1) & 3] + (m & 1)))
    peers = [(blk ^ m, rep) for m in masks]

    barrier = pltpu.get_barrier_semaphore()

    def hail(device):
        pl.semaphore_signal(barrier, inc=1, device_id=device, device_id_type=MESH)

    def if_slot(s, action):
        if s < 2:
            action()
        else:
            pl.when(halves)(action)

    def hail_sources(s):
        def action():
            for m in range(1, 8):
                hail(member(slot_cols[s], (me + m) & 7))
            if s == 0:
                pl.when(jnp.logical_not(own_pair))(lambda: hail(member(slot_cols[s], me)))
            else:
                hail(member(slot_cols[s], me))
        return action

    for s in range(4):
        if_slot(s, hail_sources(s))
    loads = [
        pltpu.make_async_copy(a, b, load.at[n])
        for n, (a, b) in enumerate(
            [
                (points_hbm, points_ref), (length_hbm, length_ref), (dir_hbm, dir_ref),
                (noise_hbm, noise_ref), (sol_hbm, sol_ref), (res_hbm, res_ref),
            ]
        )
    ]
    for copy in loads:
        copy.start()


    for copy in loads[:3]:
        copy.wait()
    row = lax.broadcasted_iota(jnp.int32, (32, 32), 0)
    lane = lax.broadcasted_iota(jnp.int32, (32, 32), 1)
    length = jnp.sum(jnp.where(row == lane, length_ref[...], 0.0), axis=1, keepdims=True)
    mine[...] = (points_ref[...] * (SCALE / length)).astype(bf16)
    direction = dir_ref[...]
    mydir[...] = jnp.concatenate(
        [direction[:, c * 256 : (c + 1) * 256] for c in range(4)], axis=0
    ).astype(bf16)

    pl.semaphore_wait(barrier, len(USES) - jnp.where(own_pair, 1, 0))

    def remote(src, dst, send_sem, recv_sem, device):
        return pltpu.make_async_remote_copy(
            src_ref=src, dst_ref=dst, send_sem=send_sem, recv_sem=recv_sem,
            device_id=device, device_id_type=MESH,
        )

    def deliver(src, dst, send_sem, recv_sem, device, is_self):
        def away():
            remote(src, dst, send_sem, recv_sem, device).start()

        if is_self is None:
            away()
        else:
            pl.when(is_self)(lambda: pltpu.make_async_copy(src, dst, recv_sem).start())
            pl.when(jnp.logical_not(is_self))(away)

    def drain(ref, sem):
        pltpu.make_async_copy(ref, ref, sem).wait()

    def drain_either(alone, ref, count, sem):
        pl.when(alone)(lambda: drain(ref.at[pl.ds(0, count - 1)], sem))
        pl.when(jnp.logical_not(alone))(lambda: drain(ref.at[pl.ds(0, count)], sem))

    def dirs_out(second_pairs):
        for u in URGENT:
            m, s, dx, dz = USES[u]
            if (s > 1) == second_pairs:
                deliver(
                    mydir, dirs.at[s * 8 + me], dir_send.at[0], dir_recv.at[s * 2 + ylo], users[u],
                    me == m if (dx, dz) == (0, 0) else None,
                )

    def points_out(r, y, second_pairs):
        def action():
            for u in URGENT:
                m, s, dx, dz = USES[u]
                if m == y * 4 + r and (s > 1) == second_pairs:
                    place = s * 2 + ylo
                    deliver(
                        mine, pts.at[place, pl.ds(0, 32)], pts_send.at[0], pts_recv.at[place], users[u],
                        me == m if (dx, dz) == (0, 0) else None,
                    )
        return action

    dirs_out(False)
    for r in range(4):
        for own in range(2):
            for y in range(2):
                pl.when(jnp.logical_and(rep == r, ylo == (y if own else 1 - y)))(points_out(r, y, False))
    dirs_out(True)
    for r in range(4):
        for y in range(2):
            if any(m == y * 4 + r and s > 1 for m, s, *_ in USES):
                pl.when(rep == r)(points_out(r, y, True))
    first[...] = jnp.zeros_like(first)
    second[...] = jnp.zeros_like(second)

    def augment(place):
        drain(pts.at[place, pl.ds(0, 32)], pts_recv.at[place])
        high, mid, low = squares(pts[place, 0:32, :])
        one = jnp.ones((1, BLOCK), f32)
        extra = jnp.concatenate([high, mid, low, one, one, one, jnp.zeros((10, BLOCK), f32)], axis=0)
        pts[place, 32:48, :] = extra.astype(bf16)

    def left_rows(place, y):
        q = pts[place, 0:32, :]
        high, mid, low = squares(q)
        one = jnp.ones((1, BLOCK), f32)
        whole = jnp.concatenate(
            [q.astype(f32) * -2.0, one, one, one, high, mid, low, jnp.zeros((10, BLOCK), f32)], axis=0
        )
        amat[y] = jnp.transpose(whole).astype(bf16)

    def spread(place):
        drain(dirs.at[pl.ds(place * 4, 4)], dir_recv.at[place])
        pieces = [dirs[place * 4 + r].astype(f32) for r in range(4)]
        for c in range(4):
            rows = jnp.concatenate([p[c * 4 : c * 4 + 4, :] for p in pieces], axis=0)
            dmat[place, :, c * 256 : (c + 1) * 256] = rows.astype(bf16)

    def pack(place, whole):
        for r in range(4):
            piece = [whole[r * 4 : r * 4 + 4, c * 256 : (c + 1) * 256] for c in range(4)]
            parts[place * 4 + r] = jnp.concatenate(piece, axis=0).astype(bf16)

    def parts_out(s, y):
        def action():
            for m in (2, 3, 1, 0):
                r = (me ^ m) & 3
                deliver(
                    parts.at[s * 8 + y * 4 + r], got.at[slot_use[s]], part_send.at[s], part_recv.at[0],
                    member(slot_cols[s], y * 4 + r),
                    jnp.logical_and(own_pair, ylo == y) if s == 0 and m == 0 else None,
                )
        return action

    def phase(ph, carry):
        diag = jnp.logical_and(own_pair, ph == 0)
        full = jnp.logical_not(jnp.logical_or(halves, diag))
        again = jnp.logical_and(own_pair, ph == 1)
        left = jnp.where(own_pair, 0, ph * 4)
        right = jnp.where(own_pair, ph * 2, ph * 4 + 2)
        near = 1 - ylo

        def left_points(b):
            @pl.when(jnp.logical_not(again))
            def _():
                augment(left + b)
                left_rows(left + b, b)

        def right_points(b):
            pl.when(jnp.logical_not(diag))(lambda: augment(right + b))

        def left_dirs(b):
            pl.when(jnp.logical_not(again))(lambda: spread(left + b))

        def right_dirs(b):
            pl.when(jnp.logical_not(diag))(lambda: spread(right + b))

        for take in (left_points, right_points, left_dirs, right_dirs):
            take(near)

        @pl.when(jnp.logical_not(full))
        def _():
            for take in (left_points, right_points, left_dirs, right_dirs):
                take(ylo)

        low_col = jnp.where(ph == 0, slot_cols[0], slot_cols[2])
        high_col = jnp.where(ph == 0, slot_cols[1], slot_cols[3])
        early = jnp.where(low_col < high_col, 0, 1)
        count = jnp.where(
            full, 32, jnp.where(diag, jnp.where(me == OWN[0], 8, 12), jnp.where(ph == 0, 16, 8))
        )
        skip = jnp.where(jnp.logical_and(me == HALVES[0], ph == 1), 8, 0)

        def tile(t):
            h = t + skip
            half_i = jnp.where(h < 8, h >> 2, 2 * early + ((h >> 2) & 1))
            half_j = jnp.where(h < 8, 4, 4 * early) + (h & 3)
            w = t >> 1
            diag_i = jnp.where(me == OWN[0], w, jnp.where(w < 3, 0, jnp.where(w < 5, 1, 2)))
            diag_j = jnp.where(me == OWN[0], w, jnp.where(w < 3, w + 1, jnp.where(w < 5, w - 1, 3)))
            i = jnp.where(full, 2 * ((t >> 4) ^ near) + ((t >> 2) & 1), jnp.where(diag, diag_i, half_i))
            j = jnp.where(full, 4 * (((t >> 3) & 1) ^ near) + (t & 3), jnp.where(diag, diag_j * 2 + (t & 1), half_j))
            return i, j, jnp.logical_and(diag, me == OWN[0])

        def place(t):
            i, j, same = tile(t)
            i0 = pl.multiple_of((i & 1) * ROWS, ROWS)
            j0 = pl.multiple_of((j & 3) * COLS, COLS)
            return i >> 1, i0, j >> 2, j0, same

        def distances(t, out):
            ib, i0, jb, j0, same = place(jnp.minimum(t, count - 1))
            out[...] = jnp.dot(
                amat[ib, pl.ds(i0, ROWS), :], pts[right + jb, :, pl.ds(j0, COLS)], preferred_element_type=f32
            )

        def products(t, dist):
            ib, i0, jb, j0, same = place(t)
            values = matern(dist[...])
            weight = jnp.where(same, 0.5, 1.0).astype(bf16)
            di = dmat[left + ib, :, pl.ds(i0, ROWS)] * weight
            dj = dmat[right + jb, :, pl.ds(j0, COLS)] * weight
            first[left + ib, :, pl.ds(i0, ROWS)] += lax.dot_general(
                dj, values, (((1,), (1,)), ((), ())), preferred_element_type=f32
            )
            second[right + jb, :, pl.ds(j0, COLS)] += jnp.dot(di, values, preferred_element_type=f32)

        distances(0, even)

        def step(n, carry):
            for m in range(2):
                t = n * 4 + m * 2
                distances(t + 1, odd)
                products(t, even)
                distances(t + 2, even)
                products(t + 1, odd)
            return carry

        def finish(side, b):
            slot = (right if side else left) >> 1
            pack(slot * 2 + b, first[slot * 2 + b] + second[slot * 2 + b])
            for s in (side, 2 + side):
                pl.when(slot == s)(parts_out(s, b))

        def segment(q, carry):
            for n, take in ((1, right_points), (2, right_dirs), (3, left_points), (4, left_dirs)):
                pl.when(jnp.logical_and(full, q == n))(lambda: take(ylo))
            lax.fori_loop(jnp.where(full, q, 0), jnp.where(full, q + 1, count >> 2), step, 0)

            @pl.when(jnp.logical_and(full, q == 3))
            def _():
                finish(0, near)

            @pl.when(jnp.logical_and(full, q == 5))
            def _():
                finish(1, near)

            return carry

        lax.fori_loop(0, jnp.where(full, 8, 1), segment, 0)
        @pl.when(jnp.logical_not(diag))
        def _():
            finish(0, ylo)
            finish(1, ylo)

        @pl.when(halves)
        def _():
            finish(0, near)
            finish(1, near)

        return carry

    lax.fori_loop(0, jnp.where(jnp.logical_or(own_pair, halves), 2, 1), phase, 0)

    for copy in loads[3:]:
        copy.wait()
    residual = res_ref[...]

    total = jnp.zeros((16, 256), f32)
    drain(got, part_recv.at[0])
    for u in range(len(USES)):
        total += got[u].astype(f32)
    product = jnp.concatenate([total[c * 4 : c * 4 + 4, :] for c in range(4)], axis=1)
    image = 3.0 * product + noise_ref[0] * direction

    stats = jnp.concatenate(
        [
            jnp.sum(a, axis=1, keepdims=True)
            for a in (residual * residual, direction * image, residual * image, image * image)
        ],
        axis=0,
    )
    row = lax.broadcasted_iota(jnp.int32, (16, 128), 0)
    lane = lax.broadcasted_iota(jnp.int32, (16, 128), 1)
    sums[blk] = jnp.sum(jnp.where(row == lane, stats, 0.0), axis=0, keepdims=True)
    copies = [
        remote(sums.at[blk], sums.at[blk], sum_send.at[0], sum_recv.at[0], peers[m]) for m in range(31)
    ]
    for copy in copies:
        copy.start()
    drain(sums.at[pl.ds(0, 31)], sum_recv.at[0])
    stats = jnp.sum(jnp.where(row == lane, jnp.sum(sums[...], axis=0), 0.0), axis=1, keepdims=True)
    rr, curv, cross, norm = stats[0:4], stats[4:8], stats[8:12], stats[12:16]
    alpha = rr / curv
    rr_new = jnp.maximum(rr - 2.0 * alpha * cross + alpha * alpha * norm, 0.0)
    new_res = residual - alpha * image
    out_sol[...] = sol_ref[...] + alpha * direction
    out_res[...] = new_res
    out_dir[...] = new_res + (rr_new / rr) * direction

    drain_either(own_pair, dirs, len(USES), dir_send.at[0])
    for r in range(4):
        count = sum(m % 4 == r for m, *_ in USES)

        @pl.when(rep == r)
        def _():
            drain_either(own_pair, pts.at[:, pl.ds(0, 32)], count, pts_send.at[0])

    for s in range(4):
        if s == 0:
            drain_either(own_pair, parts, 8, part_send.at[s])
        else:
            if_slot(s, lambda: drain(parts.at[pl.ds(0, 8)], part_send.at[s]))
    drain(sums.at[pl.ds(0, 31)], sum_send.at[0])


def store(a, b, c, out_a, out_b, out_c, sem):
    copies = [
        pltpu.make_async_copy(src, dst, sem.at[n])
        for n, (src, dst) in enumerate([(a, out_a), (b, out_b), (c, out_c)])
    ]
    for copy in copies:
        copy.start()
    for copy in copies:
        copy.wait()


def on_device(points, lengthscale, noise, solution, residual, direction):
    vmem = pl.BlockSpec(memory_space=pltpu.VMEM)
    hbm = pl.BlockSpec(memory_space=pltpu.HBM)
    dma = pltpu.SemaphoreType.DMA
    probes = direction.shape[0]
    results = pl.pallas_call(
        kernel,
        out_shape=[jax.ShapeDtypeStruct(direction.shape, f32)] * 3,
        in_specs=[hbm] * 6,
        out_specs=[vmem] * 3,
        scratch_shapes=[
            pltpu.VMEM((32, BLOCK), f32),
            pltpu.VMEM((1, 32), f32),
            pltpu.SMEM((1,), f32),
            pltpu.VMEM((probes, BLOCK), f32),
            pltpu.VMEM((probes, BLOCK), f32),
            pltpu.VMEM((probes, BLOCK), f32),
            pltpu.VMEM((32, BLOCK), bf16),
            pltpu.VMEM((16, 256), bf16),
            pltpu.VMEM((8, 48, BLOCK), bf16),
            pltpu.VMEM((32, 16, 256), bf16),
            pltpu.VMEM((8, 16, BLOCK), bf16),
            pltpu.VMEM((2, BLOCK, 48), bf16),
            pltpu.VMEM((ROWS, COLS), f32),
            pltpu.VMEM((ROWS, COLS), f32),
            pltpu.VMEM((8, 16, BLOCK), f32),
            pltpu.VMEM((8, 16, BLOCK), f32),
            pltpu.VMEM((32, 16, 256), bf16),
            pltpu.VMEM((len(USES), 16, 256), bf16),
            pltpu.VMEM((32, 1, 128), f32),
            dma((6,)), dma((1,)), dma((8,)), dma((1,)), dma((8,)), dma((4,)), dma((1,)), dma((1,)), dma((1,)),
        ],
        compiler_params=pltpu.CompilerParams(
            collective_id=0, has_side_effects=True
        ),
        cost_estimate=pl.CostEstimate(flops=2**31, bytes_accessed=2**20, transcendentals=2**23),
    )(points, lengthscale.reshape(1, 32), noise, solution, residual, direction)
    return pl.pallas_call(
        store,
        out_shape=[jax.ShapeDtypeStruct(direction.shape, f32)] * 3,
        in_specs=[vmem] * 3,
        out_specs=[hbm] * 3,
        scratch_shapes=[dma((3,))],
    )(*results)


def solution(mesh):
    in_specs = (P(None, "blk"), P(), P(), P("rep", "blk"), P("rep", "blk"), P("rep", "blk"))
    out_specs = (P("rep", "blk"), P("rep", "blk"), P("rep", "blk"))
    return jax.shard_map(
        on_device, mesh=mesh, in_specs=in_specs, out_specs=out_specs, check_vma=False
    )
```

```python
import math

import jax
import jax.numpy as jnp
from jax import lax
from jax.experimental import pallas as pl
from jax.experimental.pallas import tpu as pltpu
from jax.sharding import PartitionSpec as P

MESH = pl.DeviceIdType.MESH
bf16 = jnp.bfloat16
f32 = jnp.float32
BLOCK = 1024
ROWS = 512
COLS = 256
SCALE = math.sqrt(5.0) / 3.0
SLOTS = (
    ((-1, 0), (1, 0), (-1, -1), (1, 1)),
    ((0, 0), (1, 1), None, None),
    ((0, 0), (0, 1), None, None),
    ((0, 0), (1, 0), None, None),
    ((0, -1), (1, 1), None, None),
    ((0, 0), (1, -1), None, None),
    ((-1, 0), (1, 1), None, None),
    ((0, -1), (0, 1), (-1, 0), (1, 0)),
)
OWN = (2, 3)
HALVES = (0, 7)
USES = tuple((m, s) + SLOTS[m][s] for m in range(8) for s in range(4) if SLOTS[m][s] is not None)
URGENT = sorted(range(len(USES)), key=lambda u: (USES[u][1] > 1, -abs(USES[u][2]) - abs(USES[u][3])))


def use_of(m, s):
    for index, use in enumerate(USES):
        if use[:2] == (m, s):
            return index
    return 0


def matern(dist):
    dist = jnp.maximum(dist, 1e-30)
    root = dist * lax.rsqrt(dist)
    decay = jnp.exp2(root * (-3.0 / math.log(2.0)))
    return ((root + dist + 1.0 / 3.0) * decay).astype(bf16)


def pick(index, values):
    result = jnp.int32(values[0])
    for k in range(1, len(values)):
        if values[k] != values[0]:
            result = jnp.where(index == k, jnp.int32(values[k]), result)
    return result


def squares(points):
    wide = points.astype(f32)
    total = jnp.sum(wide * wide, axis=0, keepdims=True)
    high = total.astype(bf16).astype(f32)
    rest = total - high
    mid = rest.astype(bf16).astype(f32)
    return (high, mid, rest - mid)


def kernel(
    points_hbm, length_hbm, noise_hbm, sol_hbm, res_hbm, dir_hbm,
    out_sol, out_res, out_dir,
    points_ref, length_ref, noise_ref, sol_ref, res_ref, dir_ref,
    mine, mydir, pts, dirs, dmat, amat, even, odd, first, second, parts, got, sums,
    load, pts_send, pts_recv, dir_send, dir_recv, part_send, part_recv, sum_send, sum_recv,
):
    blk = lax.axis_index("blk")
    rep = lax.axis_index("rep")
    ylo = blk & 1
    col = blk >> 1
    x = col >> 2
    z = col & 3
    me = ylo * 4 + rep

    def column(dx, dz):
        return ((x + dx + 4) & 3) * 4 + ((z + dz + 4) & 3)

    def member(c, k):
        return (c * 2 + (k >> 2), k & 3)

    def slot_column(s):
        offsets = [SLOTS[m][s] or (0, 0) for m in range(8)]
        return column(pick(me, [d[0] for d in offsets]), pick(me, [d[1] for d in offsets]))

    slot_cols = [slot_column(s) for s in range(4)]
    slot_use = [pick(me, [use_of(m, s) for m in range(8)]) for s in range(4)]
    own_pair = jnp.logical_or(me == OWN[0], me == OWN[1])
    has_own = jnp.bool_(False)
    for m in range(8):
        if SLOTS[m][0] == (0, 0):
            has_own = jnp.logical_or(has_own, me == m)
    halves = jnp.logical_or(me == HALVES[0], me == HALVES[1])
    users = [member(column(-dx, -dz), m) for m, s, dx, dz in USES]
    hops = (0, 1, 2, 1)
    masks = sorted(range(1, 32), key=lambda m: -(hops[m >> 3] + hops[(m >> 1) & 3] + (m & 1)))
    peers = [(blk ^ m, rep) for m in masks]

    barrier = pltpu.get_barrier_semaphore()

    def hail(device):
        pl.semaphore_signal(barrier, inc=1, device_id=device, device_id_type=MESH)

    def if_slot(s, action):
        if s < 2:
            action()
        else:
            pl.when(halves)(action)

    def hail_sources(s, far):
        def action():
            for m in (2, 3) if far else (6, 7, 4, 5, 1):
                hail(member(slot_cols[s], me ^ m))
            if not far and s == 0:
                pl.when(jnp.logical_not(has_own))(lambda: hail(member(slot_cols[s], me)))
            elif not far:
                hail(member(slot_cols[s], me))
        return action

    for far in (True, False):
        for s in range(4):
            if_slot(s, hail_sources(s, far))
    loads = [
        pltpu.make_async_copy(a, b, load.at[n])
        for n, (a, b) in enumerate(
            [
                (points_hbm, points_ref), (length_hbm, length_ref), (dir_hbm, dir_ref),
                (noise_hbm, noise_ref), (sol_hbm, sol_ref), (res_hbm, res_ref),
            ]
        )
    ]
    for copy in loads:
        copy.start()


    for copy in loads[:3]:
        copy.wait()
    row = lax.broadcasted_iota(jnp.int32, (32, 32), 0)
    lane = lax.broadcasted_iota(jnp.int32, (32, 32), 1)
    length = jnp.sum(jnp.where(row == lane, length_ref[...], 0.0), axis=1, keepdims=True)
    mine[...] = (points_ref[...] * (SCALE / length)).astype(bf16)
    direction = dir_ref[...]
    mydir[...] = jnp.concatenate(
        [direction[:, c * 256 : (c + 1) * 256] for c in range(4)], axis=0
    ).astype(bf16)

    pl.semaphore_wait(barrier, len(USES) - jnp.where(has_own, 1, 0))

    def remote(src, dst, send_sem, recv_sem, device):
        return pltpu.make_async_remote_copy(
            src_ref=src, dst_ref=dst, send_sem=send_sem, recv_sem=recv_sem,
            device_id=device, device_id_type=MESH,
        )

    def deliver(src, dst, send_sem, recv_sem, device, is_self):
        def away():
            remote(src, dst, send_sem, recv_sem, device).start()

        if is_self is None:
            away()
        else:
            pl.when(is_self)(lambda: pltpu.make_async_copy(src, dst, recv_sem).start())
            pl.when(jnp.logical_not(is_self))(away)

    def drain(ref, sem):
        pltpu.make_async_copy(ref, ref, sem).wait()

    def drain_either(alone, ref, count, sem):
        pl.when(alone)(lambda: drain(ref.at[pl.ds(0, count - 1)], sem))
        pl.when(jnp.logical_not(alone))(lambda: drain(ref.at[pl.ds(0, count)], sem))

    def dirs_out(second_pairs):
        for u in URGENT:
            m, s, dx, dz = USES[u]
            if (s > 1) == second_pairs:
                deliver(
                    mydir, dirs.at[s * 8 + me], dir_send.at[0], dir_recv.at[s * 2 + ylo], users[u],
                    me == m if (dx, dz) == (0, 0) else None,
                )

    def points_out(r, y, second_pairs):
        def action():
            for u in URGENT:
                m, s, dx, dz = USES[u]
                if m == y * 4 + r and (s > 1) == second_pairs:
                    place = s * 2 + ylo
                    deliver(
                        mine, pts.at[place, pl.ds(0, 32)], pts_send.at[0], pts_recv.at[place], users[u],
                        me == m if (dx, dz) == (0, 0) else None,
                    )
        return action

    dirs_out(False)
    for r in range(4):
        for own in range(2):
            for y in range(2):
                pl.when(jnp.logical_and(rep == r, ylo == (y if own else 1 - y)))(points_out(r, y, False))
    dirs_out(True)
    for r in range(4):
        for y in range(2):
            if any(m == y * 4 + r and s > 1 for m, s, *_ in USES):
                pl.when(rep == r)(points_out(r, y, True))
    first[...] = jnp.zeros_like(first)
    second[...] = jnp.zeros_like(second)

    def augment(place):
        drain(pts.at[place, pl.ds(0, 32)], pts_recv.at[place])
        high, mid, low = squares(pts[place, 0:32, :])
        one = jnp.ones((1, BLOCK), f32)
        extra = jnp.concatenate([high, mid, low, one, one, one, jnp.zeros((10, BLOCK), f32)], axis=0)
        pts[place, 32:48, :] = extra.astype(bf16)

    def left_rows(place, y):
        q = pts[place, 0:32, :]
        high, mid, low = squares(q)
        one = jnp.ones((1, BLOCK), f32)
        whole = jnp.concatenate(
            [q.astype(f32) * -2.0, one, one, one, high, mid, low, jnp.zeros((10, BLOCK), f32)], axis=0
        )
        amat[y] = jnp.transpose(whole).astype(bf16)

    def spread(place):
        drain(dirs.at[pl.ds(place * 4, 4)], dir_recv.at[place])
        pieces = [dirs[place * 4 + r].astype(f32) for r in range(4)]
        for c in range(4):
            rows = jnp.concatenate([p[c * 4 : c * 4 + 4, :] for p in pieces], axis=0)
            dmat[place, :, c * 256 : (c + 1) * 256] = rows.astype(bf16)

    def pack(place, whole):
        for r in range(4):
            piece = [whole[r * 4 : r * 4 + 4, c * 256 : (c + 1) * 256] for c in range(4)]
            parts[place * 4 + r] = jnp.concatenate(piece, axis=0).astype(bf16)

    def parts_out(s, y):
        def action():
            for m in (2, 3, 1, 0):
                r = (me ^ m) & 3
                deliver(
                    parts.at[s * 8 + y * 4 + r], got.at[slot_use[s]], part_send.at[s], part_recv.at[0],
                    member(slot_cols[s], y * 4 + r),
                    jnp.logical_and(has_own, ylo == y) if s == 0 and m == 0 else None,
                )
        return action

    def phase(ph, carry):
        diag = jnp.logical_and(own_pair, ph == 0)
        full = jnp.logical_not(jnp.logical_or(halves, diag))
        again = jnp.logical_and(own_pair, ph == 1)
        left = jnp.where(own_pair, 0, ph * 4)
        right = jnp.where(own_pair, ph * 2, ph * 4 + 2)
        near = 1 - ylo

        def left_points(b):
            @pl.when(jnp.logical_not(again))
            def _():
                augment(left + b)
                left_rows(left + b, b)

        def right_points(b):
            pl.when(jnp.logical_not(diag))(lambda: augment(right + b))

        def left_dirs(b):
            pl.when(jnp.logical_not(again))(lambda: spread(left + b))

        def right_dirs(b):
            pl.when(jnp.logical_not(diag))(lambda: spread(right + b))

        for take in (left_points, right_points, left_dirs, right_dirs):
            take(near)

        @pl.when(jnp.logical_not(full))
        def _():
            for take in (left_points, right_points, left_dirs, right_dirs):
                take(ylo)

        low_col = jnp.where(ph == 0, slot_cols[0], slot_cols[2])
        high_col = jnp.where(ph == 0, slot_cols[1], slot_cols[3])
        early = jnp.where(low_col < high_col, 0, 1)
        count = jnp.where(
            full, 32, jnp.where(diag, jnp.where(me == OWN[0], 8, 16), jnp.where((ph == 0) == (me == HALVES[1]), 16, 8))
        )
        skip = jnp.where(jnp.logical_and(me == HALVES[0], ph == 0), 8, 0)

        def tile(t):
            h = t + skip
            half_i = jnp.where(h < 8, h >> 2, 2 * early + ((h >> 2) & 1))
            half_j = jnp.where(h < 8, 4, 4 * early) + (h & 3)
            w = t >> 1
            diag_i = jnp.where(me == OWN[0], w, jnp.where(w < 3, 0, jnp.where(w < 5, 1, 2)))
            diag_j = jnp.where(me == OWN[0], w, jnp.where(w < 3, w + 1, jnp.where(w < 5, w - 1, 3)))
            i = jnp.where(full, 2 * ((t >> 4) ^ near) + ((t >> 2) & 1), jnp.where(diag, diag_i, half_i))
            j = jnp.where(full, 4 * (((t >> 3) & 1) ^ near) + (t & 3), jnp.where(diag, diag_j * 2 + (t & 1), half_j))
            return i, j, jnp.logical_and(diag, me == OWN[0])

        def place(t):
            i, j, same = tile(t)
            i0 = pl.multiple_of((i & 1) * ROWS, ROWS)
            j0 = pl.multiple_of((j & 3) * COLS, COLS)
            return i >> 1, i0, j >> 2, j0, same

        def distances(t, out):
            ib, i0, jb, j0, same = place(jnp.minimum(t, count - 1))
            out[...] = jnp.dot(
                amat[ib, pl.ds(i0, ROWS), :], pts[right + jb, :, pl.ds(j0, COLS)], preferred_element_type=f32
            )

        def products(t, dist):
            ib, i0, jb, j0, same = place(t)
            values = matern(dist[...])
            weight = jnp.where(same, 0.5, jnp.where(jnp.logical_and(diag, t >= 12), 0.0, 1.0)).astype(bf16)
            di = dmat[left + ib, :, pl.ds(i0, ROWS)] * weight
            dj = dmat[right + jb, :, pl.ds(j0, COLS)] * weight
            first[left + ib, :, pl.ds(i0, ROWS)] += lax.dot_general(
                dj, values, (((1,), (1,)), ((), ())), preferred_element_type=f32
            )
            second[right + jb, :, pl.ds(j0, COLS)] += jnp.dot(di, values, preferred_element_type=f32)

        distances(0, even)

        def step(n, carry):
            for m in range(4):
                t = n * 8 + m * 2
                distances(t + 1, odd)
                products(t, even)
                distances(t + 2, even)
                products(t + 1, odd)
            return carry

        def finish(side, b):
            slot = (right if side else left) >> 1
            pack(slot * 2 + b, first[slot * 2 + b] + second[slot * 2 + b])
            for s in (side, 2 + side):
                pl.when(slot == s)(parts_out(s, b))

        def segment(q, carry):
            for n, take in ((0, right_points), (1, right_dirs), (1, left_points), (2, left_dirs)):
                pl.when(jnp.logical_and(full, q == n))(lambda: take(ylo))
            lax.fori_loop(jnp.where(full, q, 0), jnp.where(full, q + 1, count >> 3), step, 0)

            @pl.when(jnp.logical_and(full, q == 1))
            def _():
                finish(0, near)

            @pl.when(jnp.logical_and(full, q == 2))
            def _():
                finish(1, near)

            return carry

        lax.fori_loop(0, jnp.where(full, 4, 1), segment, 0)
        @pl.when(jnp.logical_not(diag))
        def _():
            finish(0, ylo)
            finish(1, ylo)

        @pl.when(halves)
        def _():
            finish(0, near)
            finish(1, near)

        return carry

    lax.fori_loop(0, jnp.where(jnp.logical_or(own_pair, halves), 2, 1), phase, 0)

    for copy in loads[3:]:
        copy.wait()
    residual = res_ref[...]

    total = jnp.zeros((16, 256), f32)
    drain(got, part_recv.at[0])
    for u in range(len(USES)):
        total += got[u].astype(f32)
    product = jnp.concatenate([total[c * 4 : c * 4 + 4, :] for c in range(4)], axis=1)
    image = 3.0 * product + noise_ref[0] * direction

    stats = jnp.concatenate(
        [
            jnp.sum(a, axis=1, keepdims=True)
            for a in (residual * residual, direction * image, residual * image, image * image)
        ],
        axis=0,
    )
    row = lax.broadcasted_iota(jnp.int32, (16, 128), 0)
    lane = lax.broadcasted_iota(jnp.int32, (16, 128), 1)
    sums[blk] = jnp.sum(jnp.where(row == lane, stats, 0.0), axis=0, keepdims=True)
    copies = [
        remote(sums.at[blk], sums.at[blk], sum_send.at[0], sum_recv.at[0], peers[m]) for m in range(31)
    ]
    for copy in copies:
        copy.start()
    drain(sums.at[pl.ds(0, 31)], sum_recv.at[0])
    stats = jnp.sum(jnp.where(row == lane, jnp.sum(sums[...], axis=0), 0.0), axis=1, keepdims=True)
    rr, curv, cross, norm = stats[0:4], stats[4:8], stats[8:12], stats[12:16]
    alpha = rr / curv
    rr_new = jnp.maximum(rr - 2.0 * alpha * cross + alpha * alpha * norm, 0.0)
    new_res = residual - alpha * image
    out_sol[...] = sol_ref[...] + alpha * direction
    out_res[...] = new_res
    out_dir[...] = new_res + (rr_new / rr) * direction

    drain_either(has_own, dirs, len(USES), dir_send.at[0])
    for r in range(4):
        count = sum(m % 4 == r for m, *_ in USES)

        @pl.when(rep == r)
        def _():
            drain_either(has_own, pts.at[:, pl.ds(0, 32)], count, pts_send.at[0])

    for s in range(4):
        if s == 0:
            drain_either(has_own, parts, 8, part_send.at[s])
        else:
            if_slot(s, lambda: drain(parts.at[pl.ds(0, 8)], part_send.at[s]))
    drain(sums.at[pl.ds(0, 31)], sum_send.at[0])


def store(a, b, c, out_a, out_b, out_c, sem):
    copies = [
        pltpu.make_async_copy(src, dst, sem.at[n])
        for n, (src, dst) in enumerate([(a, out_a), (b, out_b), (c, out_c)])
    ]
    for copy in copies:
        copy.start()
    for copy in copies:
        copy.wait()


def on_device(points, lengthscale, noise, solution, residual, direction):
    vmem = pl.BlockSpec(memory_space=pltpu.VMEM)
    hbm = pl.BlockSpec(memory_space=pltpu.HBM)
    dma = pltpu.SemaphoreType.DMA
    probes = direction.shape[0]
    results = pl.pallas_call(
        kernel,
        out_shape=[jax.ShapeDtypeStruct(direction.shape, f32)] * 3,
        in_specs=[hbm] * 6,
        out_specs=[vmem] * 3,
        scratch_shapes=[
            pltpu.VMEM((32, BLOCK), f32),
            pltpu.VMEM((1, 32), f32),
            pltpu.SMEM((1,), f32),
            pltpu.VMEM((probes, BLOCK), f32),
            pltpu.VMEM((probes, BLOCK), f32),
            pltpu.VMEM((probes, BLOCK), f32),
            pltpu.VMEM((32, BLOCK), bf16),
            pltpu.VMEM((16, 256), bf16),
            pltpu.VMEM((8, 48, BLOCK), bf16),
            pltpu.VMEM((32, 16, 256), bf16),
            pltpu.VMEM((8, 16, BLOCK), bf16),
            pltpu.VMEM((2, BLOCK, 48), bf16),
            pltpu.VMEM((ROWS, COLS), f32),
            pltpu.VMEM((ROWS, COLS), f32),
            pltpu.VMEM((8, 16, BLOCK), f32),
            pltpu.VMEM((8, 16, BLOCK), f32),
            pltpu.VMEM((32, 16, 256), bf16),
            pltpu.VMEM((len(USES), 16, 256), bf16),
            pltpu.VMEM((32, 1, 128), f32),
            dma((6,)), dma((1,)), dma((8,)), dma((1,)), dma((8,)), dma((4,)), dma((1,)), dma((1,)), dma((1,)),
        ],
        compiler_params=pltpu.CompilerParams(
            collective_id=0, has_side_effects=True
        ),
        cost_estimate=pl.CostEstimate(flops=2**31, bytes_accessed=2**20, transcendentals=2**23),
    )(points, lengthscale.reshape(1, 32), noise, solution, residual, direction)
    return pl.pallas_call(
        store,
        out_shape=[jax.ShapeDtypeStruct(direction.shape, f32)] * 3,
        in_specs=[vmem] * 3,
        out_specs=[hbm] * 3,
        scratch_shapes=[dma((3,))],
    )(*results)


def solution(mesh):
    in_specs = (P(None, "blk"), P(), P(), P("rep", "blk"), P("rep", "blk"), P("rep", "blk"))
    out_specs = (P("rep", "blk"), P("rep", "blk"), P("rep", "blk"))
    return jax.shard_map(
        on_device, mesh=mesh, in_specs=in_specs, out_specs=out_specs, check_vma=False
    )
```

```python
import functools
import math

import jax
import jax.numpy as jnp
from jax import lax
from jax.experimental import pallas as pl
from jax.experimental.pallas import tpu as pltpu
from jax.sharding import PartitionSpec as P

MESH = pl.DeviceIdType.MESH
bf16 = jnp.bfloat16
f32 = jnp.float32
BLOCK = 1024
ROWS = 512
COLS = 256
SCALE = math.sqrt(5.0) / 3.0
SLOTS = (
    ((-1, 0), (1, 0), (-1, -1), (1, 1)),
    ((0, 0), (1, 1), None, None),
    ((0, 0), (0, 1), None, None),
    ((0, 0), (1, 0), None, None),
    ((0, -1), (1, 1), None, None),
    ((0, 0), (1, -1), None, None),
    ((-1, 0), (1, 1), None, None),
    ((0, -1), (0, 1), (-1, 0), (1, 0)),
)
OWN = (2, 3)
HALVES = (0, 7)
USES = tuple((m, s) + SLOTS[m][s] for m in range(8) for s in range(4) if SLOTS[m][s] is not None)
URGENT = sorted(range(len(USES)), key=lambda u: (USES[u][1] > 1, -abs(USES[u][2]) - abs(USES[u][3])))


def use_of(m, s):
    for index, use in enumerate(USES):
        if use[:2] == (m, s):
            return index
    return 0


def matern(dist):
    dist = jnp.maximum(dist, 1e-30)
    root = dist * lax.rsqrt(dist)
    decay = jnp.exp2(root * (-3.0 / math.log(2.0)))
    return ((root + dist + 1.0 / 3.0) * decay).astype(bf16)


def pick(index, values):
    result = jnp.int32(values[0])
    for k in range(1, len(values)):
        if values[k] != values[0]:
            result = jnp.where(index == k, jnp.int32(values[k]), result)
    return result


def squares(points):
    wide = points.astype(f32)
    total = jnp.sum(wide * wide, axis=0, keepdims=True)
    high = total.astype(bf16).astype(f32)
    rest = total - high
    mid = rest.astype(bf16).astype(f32)
    return (high, mid, rest - mid)


def kernel(
    points_hbm, length_hbm, noise_hbm, sol_hbm, res_hbm, dir_hbm,
    out_sol, out_res, out_dir,
    points_ref, length_ref, noise_ref, sol_ref, res_ref, dir_ref,
    mine, mydir, pts, dirs, dmat, amat, even, odd, first, second, parts, got, sums,
    load, pts_send, pts_recv, dir_send, dir_recv, part_send, part_recv, sum_send, sum_recv,
):
    blk = lax.axis_index("blk")
    rep = lax.axis_index("rep")
    ylo = blk & 1
    col = blk >> 1
    x = col >> 2
    z = col & 3
    me = ylo * 4 + rep

    def column(dx, dz):
        return ((x + dx + 4) & 3) * 4 + ((z + dz + 4) & 3)

    def member(c, k):
        return (c * 2 + (k >> 2), k & 3)

    def slot_column(s):
        offsets = [SLOTS[m][s] or (0, 0) for m in range(8)]
        return column(pick(me, [d[0] for d in offsets]), pick(me, [d[1] for d in offsets]))

    slot_cols = [slot_column(s) for s in range(4)]
    slot_use = [pick(me, [use_of(m, s) for m in range(8)]) for s in range(4)]
    own_pair = jnp.logical_or(me == OWN[0], me == OWN[1])
    has_own = jnp.bool_(False)
    for m in range(8):
        if SLOTS[m][0] == (0, 0):
            has_own = jnp.logical_or(has_own, me == m)
    halves = jnp.logical_or(me == HALVES[0], me == HALVES[1])
    users = [member(column(-dx, -dz), m) for m, s, dx, dz in USES]
    hops = (0, 1, 2, 1)
    masks = sorted(range(1, 32), key=lambda m: -(hops[m >> 3] + hops[(m >> 1) & 3] + (m & 1)))
    peers = [(blk ^ m, rep) for m in masks]

    barrier = pltpu.get_barrier_semaphore()

    def hail(device):
        pl.semaphore_signal(barrier, inc=1, device_id=device, device_id_type=MESH)

    def if_slot(s, action):
        if s < 2:
            action()
        else:
            pl.when(halves)(action)

    def hail_sources(s, far):
        def action():
            for m in (2, 3) if far else (6, 7, 4, 5, 1):
                hail(member(slot_cols[s], me ^ m))
            if not far and s == 0:
                pl.when(jnp.logical_not(has_own))(lambda: hail(member(slot_cols[s], me)))
            elif not far:
                hail(member(slot_cols[s], me))
        return action

    for far in (True, False):
        for s in range(4):
            if_slot(s, hail_sources(s, far))
    loads = [
        pltpu.make_async_copy(a, b, load.at[n])
        for n, (a, b) in enumerate(
            [
                (points_hbm, points_ref), (length_hbm, length_ref), (dir_hbm, dir_ref),
                (noise_hbm, noise_ref), (sol_hbm, sol_ref), (res_hbm, res_ref),
            ]
        )
    ]
    for copy in loads:
        copy.start()


    for copy in loads[:3]:
        copy.wait()
    row = lax.broadcasted_iota(jnp.int32, (32, 32), 0)
    lane = lax.broadcasted_iota(jnp.int32, (32, 32), 1)
    length = jnp.sum(jnp.where(row == lane, length_ref[...], 0.0), axis=1, keepdims=True)
    mine[...] = (points_ref[...] * (SCALE / length)).astype(bf16)
    direction = dir_ref[...]
    mydir[...] = jnp.concatenate(
        [direction[:, c * 256 : (c + 1) * 256] for c in range(4)], axis=0
    ).astype(bf16)

    pl.semaphore_wait(barrier, len(USES) - jnp.where(has_own, 1, 0))

    def remote(src, dst, send_sem, recv_sem, device):
        return pltpu.make_async_remote_copy(
            src_ref=src, dst_ref=dst, send_sem=send_sem, recv_sem=recv_sem,
            device_id=device, device_id_type=MESH,
        )

    def deliver(src, dst, send_sem, recv_sem, device, is_self):
        def away():
            remote(src, dst, send_sem, recv_sem, device).start()

        if is_self is None:
            away()
        else:
            pl.when(is_self)(lambda: pltpu.make_async_copy(src, dst, recv_sem).start())
            pl.when(jnp.logical_not(is_self))(away)

    def drain(ref, sem):
        pltpu.make_async_copy(ref, ref, sem).wait()

    def drain_either(alone, ref, count, sem):
        pl.when(alone)(lambda: drain(ref.at[pl.ds(0, count - 1)], sem))
        pl.when(jnp.logical_not(alone))(lambda: drain(ref.at[pl.ds(0, count)], sem))

    def dirs_out(second_pairs):
        for u in URGENT:
            m, s, dx, dz = USES[u]
            if (s > 1) == second_pairs:
                deliver(
                    mydir, dirs.at[s * 8 + me], dir_send.at[0], dir_recv.at[s * 2 + ylo], users[u],
                    me == m if (dx, dz) == (0, 0) else None,
                )

    def points_out(r, y, second_pairs):
        def action():
            for u in URGENT:
                m, s, dx, dz = USES[u]
                if m == y * 4 + r and (s > 1) == second_pairs:
                    place = s * 2 + ylo
                    give = functools.partial(
                        deliver, mine, pts.at[place, pl.ds(0, 32)], pts_send.at[0], pts_recv.at[place], users[u],
                        me == m if (dx, dz) == (0, 0) else None,
                    )
                    if m == HALVES[1] and s > 1:
                        pl.when(ylo == s - 2)(give)
                    else:
                        give()
        return action

    dirs_out(False)
    for r in range(4):
        for own in range(2):
            for y in range(2):
                pl.when(jnp.logical_and(rep == r, ylo == (y if own else 1 - y)))(points_out(r, y, False))
    dirs_out(True)
    for r in range(4):
        for y in range(2):
            if any(m == y * 4 + r and s > 1 for m, s, *_ in USES):
                pl.when(rep == r)(points_out(r, y, True))
    first[...] = jnp.zeros_like(first)
    second[...] = jnp.zeros_like(second)

    def augment(place):
        drain(pts.at[place, pl.ds(0, 32)], pts_recv.at[place])
        high, mid, low = squares(pts[place, 0:32, :])
        one = jnp.ones((1, BLOCK), f32)
        extra = jnp.concatenate([high, mid, low, one, one, one, jnp.zeros((10, BLOCK), f32)], axis=0)
        pts[place, 32:48, :] = extra.astype(bf16)

    def left_rows(place, y):
        q = pts[place, 0:32, :]
        high, mid, low = squares(q)
        one = jnp.ones((1, BLOCK), f32)
        whole = jnp.concatenate(
            [q.astype(f32) * -2.0, one, one, one, high, mid, low, jnp.zeros((10, BLOCK), f32)], axis=0
        )
        amat[y] = jnp.transpose(whole).astype(bf16)

    def spread(place):
        drain(dirs.at[pl.ds(place * 4, 4)], dir_recv.at[place])
        pieces = [dirs[place * 4 + r].astype(f32) for r in range(4)]
        for c in range(4):
            rows = jnp.concatenate([p[c * 4 : c * 4 + 4, :] for p in pieces], axis=0)
            dmat[place, :, c * 256 : (c + 1) * 256] = rows.astype(bf16)

    def pack(place, whole):
        for r in range(4):
            piece = [whole[r * 4 : r * 4 + 4, c * 256 : (c + 1) * 256] for c in range(4)]
            parts[place * 4 + r] = jnp.concatenate(piece, axis=0).astype(bf16)

    def parts_out(s, y):
        def action():
            for m in (2, 3, 1, 0):
                r = (me ^ m) & 3
                deliver(
                    parts.at[s * 8 + y * 4 + r], got.at[slot_use[s]], part_send.at[s], part_recv.at[0],
                    member(slot_cols[s], y * 4 + r),
                    jnp.logical_and(has_own, ylo == y) if s == 0 and m == 0 else None,
                )
        return action

    def phase(ph, carry):
        diag = jnp.logical_and(own_pair, ph == 0)
        full = jnp.logical_not(jnp.logical_or(halves, diag))
        again = jnp.logical_and(own_pair, ph == 1)
        left = jnp.where(own_pair, 0, ph * 4)
        right = jnp.where(own_pair, ph * 2, ph * 4 + 2)
        near = 1 - ylo

        quarter = jnp.logical_and(me == HALVES[1], ph == 1)

        def left_points(b):
            @pl.when(jnp.logical_not(jnp.logical_or(again, jnp.logical_and(quarter, b == 1))))
            def _():
                augment(left + b)
                left_rows(left + b, b)

        def right_points(b):
            skipped = jnp.logical_or(diag, jnp.logical_and(quarter, b == 0))
            pl.when(jnp.logical_not(skipped))(lambda: augment(right + b))

        def left_dirs(b):
            pl.when(jnp.logical_not(again))(lambda: spread(left + b))

        def right_dirs(b):
            pl.when(jnp.logical_not(diag))(lambda: spread(right + b))

        for take in (left_points, right_points, left_dirs, right_dirs):
            take(near)

        @pl.when(jnp.logical_not(full))
        def _():
            for take in (left_points, right_points, left_dirs, right_dirs):
                take(ylo)

        low_col = jnp.where(ph == 0, slot_cols[0], slot_cols[2])
        high_col = jnp.where(ph == 0, slot_cols[1], slot_cols[3])
        early = jnp.where(low_col < high_col, 0, 1)
        count = jnp.where(
            full, 32, jnp.where(diag, jnp.where(me == OWN[0], 8, 16), jnp.where((ph == 0) == (me == HALVES[1]), 16, 8))
        )
        skip = jnp.where(jnp.logical_and(me == HALVES[0], ph == 0), 8, 0)

        def tile(t):
            h = t + skip
            half_i = jnp.where(h < 8, h >> 2, 2 * early + ((h >> 2) & 1))
            half_j = jnp.where(h < 8, 4, 4 * early) + (h & 3)
            w = t >> 1
            diag_i = jnp.where(me == OWN[0], w, jnp.where(w < 3, 0, jnp.where(w < 5, 1, 2)))
            diag_j = jnp.where(me == OWN[0], w, jnp.where(w < 3, w + 1, jnp.where(w < 5, w - 1, 3)))
            i = jnp.where(full, 2 * ((t >> 4) ^ near) + ((t >> 2) & 1), jnp.where(diag, diag_i, half_i))
            j = jnp.where(full, 4 * (((t >> 3) & 1) ^ near) + (t & 3), jnp.where(diag, diag_j * 2 + (t & 1), half_j))
            return i, j, jnp.logical_and(diag, me == OWN[0])

        def place(t):
            i, j, same = tile(t)
            i0 = pl.multiple_of((i & 1) * ROWS, ROWS)
            j0 = pl.multiple_of((j & 3) * COLS, COLS)
            return i >> 1, i0, j >> 2, j0, same

        def distances(t, out):
            ib, i0, jb, j0, same = place(jnp.minimum(t, count - 1))
            out[...] = jnp.dot(
                amat[ib, pl.ds(i0, ROWS), :], pts[right + jb, :, pl.ds(j0, COLS)], preferred_element_type=f32
            )

        def products(t, dist):
            ib, i0, jb, j0, same = place(t)
            values = matern(dist[...])
            weight = jnp.where(same, 0.5, jnp.where(jnp.logical_and(diag, t >= 12), 0.0, 1.0)).astype(bf16)
            di = dmat[left + ib, :, pl.ds(i0, ROWS)] * weight
            dj = dmat[right + jb, :, pl.ds(j0, COLS)] * weight
            first[left + ib, :, pl.ds(i0, ROWS)] += lax.dot_general(
                dj, values, (((1,), (1,)), ((), ())), preferred_element_type=f32
            )
            second[right + jb, :, pl.ds(j0, COLS)] += jnp.dot(di, values, preferred_element_type=f32)

        distances(0, even)

        def step(n, carry):
            for m in range(4):
                t = n * 8 + m * 2
                distances(t + 1, odd)
                products(t, even)
                distances(t + 2, even)
                products(t + 1, odd)
            return carry

        def finish(side, b):
            slot = (right if side else left) >> 1
            pack(slot * 2 + b, first[slot * 2 + b] + second[slot * 2 + b])
            for s in (side, 2 + side):
                pl.when(slot == s)(parts_out(s, b))

        def segment(q, carry):
            for n, take in ((0, right_points), (1, right_dirs), (1, left_points), (2, left_dirs)):
                pl.when(jnp.logical_and(full, q == n))(lambda: take(ylo))
            lax.fori_loop(jnp.where(full, q, 0), jnp.where(full, q + 1, count >> 3), step, 0)

            @pl.when(jnp.logical_and(full, q == 1))
            def _():
                finish(0, near)

            @pl.when(jnp.logical_and(full, q == 2))
            def _():
                finish(1, near)

            return carry

        lax.fori_loop(0, jnp.where(full, 4, 1), segment, 0)
        @pl.when(jnp.logical_not(diag))
        def _():
            finish(0, ylo)
            finish(1, ylo)

        @pl.when(halves)
        def _():
            finish(0, near)
            finish(1, near)

        return carry

    lax.fori_loop(0, jnp.where(jnp.logical_or(own_pair, halves), 2, 1), phase, 0)

    for copy in loads[3:]:
        copy.wait()
    residual = res_ref[...]

    own_rr = jnp.sum(residual * residual, axis=1, keepdims=True)
    shift = noise_ref[0] * direction
    total = jnp.zeros((16, 256), f32)
    drain(got, part_recv.at[0])
    for u in range(len(USES)):
        total += got[u].astype(f32)
    product = jnp.concatenate([total[c * 4 : c * 4 + 4, :] for c in range(4)], axis=1)
    image = 3.0 * product + shift

    stats = jnp.concatenate(
        [own_rr] + [jnp.sum(a * image, axis=1, keepdims=True) for a in (direction, residual, image)], axis=0
    )
    row = lax.broadcasted_iota(jnp.int32, (16, 128), 0)
    lane = lax.broadcasted_iota(jnp.int32, (16, 128), 1)
    sums[blk] = jnp.sum(jnp.where(row == lane, stats, 0.0), axis=0, keepdims=True)
    copies = [
        remote(sums.at[blk], sums.at[blk], sum_send.at[0], sum_recv.at[0], peers[m]) for m in range(31)
    ]
    for copy in copies:
        copy.start()
    drain(sums.at[pl.ds(0, 31)], sum_recv.at[0])
    stats = jnp.sum(jnp.where(row == lane, jnp.sum(sums[...], axis=0), 0.0), axis=1, keepdims=True)
    rr, curv, cross, norm = stats[0:4], stats[4:8], stats[8:12], stats[12:16]
    alpha = rr / curv
    rr_new = jnp.maximum(rr - 2.0 * alpha * cross + alpha * alpha * norm, 0.0)
    new_res = residual - alpha * image
    out_sol[...] = sol_ref[...] + alpha * direction
    out_res[...] = new_res
    out_dir[...] = new_res + (rr_new / rr) * direction

    drain_either(has_own, dirs, len(USES), dir_send.at[0])
    for r in range(4):
        count = sum(m % 4 == r for m, *_ in USES) - (r == HALVES[1] % 4)

        @pl.when(rep == r)
        def _():
            drain_either(has_own, pts.at[:, pl.ds(0, 32)], count, pts_send.at[0])

    for s in range(4):
        if s == 0:
            drain_either(has_own, parts, 8, part_send.at[s])
        else:
            if_slot(s, lambda: drain(parts.at[pl.ds(0, 8)], part_send.at[s]))
    drain(sums.at[pl.ds(0, 31)], sum_send.at[0])


def store(a, b, c, out_a, out_b, out_c, sem):
    copies = [
        pltpu.make_async_copy(src, dst, sem.at[n])
        for n, (src, dst) in enumerate([(a, out_a), (b, out_b), (c, out_c)])
    ]
    for copy in copies:
        copy.start()
    for copy in copies:
        copy.wait()


def on_device(points, lengthscale, noise, solution, residual, direction):
    vmem = pl.BlockSpec(memory_space=pltpu.VMEM)
    hbm = pl.BlockSpec(memory_space=pltpu.HBM)
    dma = pltpu.SemaphoreType.DMA
    probes = direction.shape[0]
    results = pl.pallas_call(
        kernel,
        out_shape=[jax.ShapeDtypeStruct(direction.shape, f32)] * 3,
        in_specs=[hbm] * 6,
        out_specs=[vmem] * 3,
        scratch_shapes=[
            pltpu.VMEM((32, BLOCK), f32),
            pltpu.VMEM((1, 32), f32),
            pltpu.SMEM((1,), f32),
            pltpu.VMEM((probes, BLOCK), f32),
            pltpu.VMEM((probes, BLOCK), f32),
            pltpu.VMEM((probes, BLOCK), f32),
            pltpu.VMEM((32, BLOCK), bf16),
            pltpu.VMEM((16, 256), bf16),
            pltpu.VMEM((8, 48, BLOCK), bf16),
            pltpu.VMEM((32, 16, 256), bf16),
            pltpu.VMEM((8, 16, BLOCK), bf16),
            pltpu.VMEM((2, BLOCK, 48), bf16),
            pltpu.VMEM((ROWS, COLS), f32),
            pltpu.VMEM((ROWS, COLS), f32),
            pltpu.VMEM((8, 16, BLOCK), f32),
            pltpu.VMEM((8, 16, BLOCK), f32),
            pltpu.VMEM((32, 16, 256), bf16),
            pltpu.VMEM((len(USES), 16, 256), bf16),
            pltpu.VMEM((32, 1, 128), f32),
            dma((6,)), dma((1,)), dma((8,)), dma((1,)), dma((8,)), dma((4,)), dma((1,)), dma((1,)), dma((1,)),
        ],
        compiler_params=pltpu.CompilerParams(
            collective_id=0, has_side_effects=True
        ),
        cost_estimate=pl.CostEstimate(flops=2**31, bytes_accessed=2**20, transcendentals=2**23),
    )(points, lengthscale.reshape(1, 32), noise, solution, residual, direction)
    return pl.pallas_call(
        store,
        out_shape=[jax.ShapeDtypeStruct(direction.shape, f32)] * 3,
        in_specs=[vmem] * 3,
        out_specs=[hbm] * 3,
        scratch_shapes=[dma((3,))],
    )(*results)


def solution(mesh):
    in_specs = (P(None, "blk"), P(), P(), P("rep", "blk"), P("rep", "blk"), P("rep", "blk"))
    out_specs = (P("rep", "blk"), P("rep", "blk"), P("rep", "blk"))
    return jax.shard_map(
        on_device, mesh=mesh, in_specs=in_specs, out_specs=out_specs, check_vma=False
    )
```
